128 devices in a mesh: row: 8 (over x_lo, z), col: 16 (over x_hi, y, core).
Axes of the slice: x: 4 (x_hi: 2, x_lo: 2; x = x_hi * 2 + x_lo), y: 4, z: 4, core: 2. Of those that a mesh axis runs over, the one named last changes fastest.
Arguments:
- inverse_block: float32 [12288, 12288], P('row', 'col'), may hold values from -0.14433757 to 0.14433757, as said below
- grid_position: int32 [12288], replicated, may hold values from 0 to 12287, each once
- panel_a: float32 [512, 12288], P('row', 'col'), may hold values from -1.5 to 1.5
- pivot_inverse_a: float32 [512, 512], replicated, may hold values from -6 to 6
- chosen_rows: int32 [8192], replicated, may hold values from 0 to 12287, as said below
- top_panel_b: float32 [512, 512], replicated, may hold values from -1.5 to 1.5
- panel_b: float32 [512, 8192], P('row', 'col'), may hold values from -1.5 to 1.5
- pivot_inverse_b: float32 [512, 512], replicated, may hold values from -6 to 6
Outputs:
- inverse_panel_a: float32 [12288, 512], P(('row', 'col'))
- diagonal_a: float32 [512, 512], replicated
- inverse_panel_b: float32 [12288, 512], P(('row', 'col'))
- inverse_top_b: float32 [512, 512], replicated
- diagonal_b: float32 [512, 512], replicated
The draws below stay inside these ranges and needn't reach their ends.
Inputs may be any that keep to these rules, and one draw needn't show every extreme that they name: `grid_position`: each of 0 to 12287 appears once. `chosen_rows`: 8192 distinct values. `inverse_block`: symmetric: entry (i, j) equals entry (j, i) in grid storage order.
All inputs are finite; a program needn't handle non-finite values.
Results may differ from the reference program's by a relative error of at most 0.00008.
Values sent between devices are 32-bit elements; how exact they have to be, the bound alone decides.
A program may use at most 128 MiB of HBM per device.

```python
import jax
import jax.numpy as jnp
from jax import lax

W = 512
M = 12288
MB = 8192
N_ROW = 8
N_COL = 16


def draw_chosen_rows(key, part):
    return jax.random.permutation(jax.random.fold_in(key, 11), M)[:MB].astype(jnp.int32)


def draw_inverse_block(key, part):
    base_key = jax.random.fold_in(key, 23)
    value_key = jax.random.fold_in(base_key, 1)
    pair_key = jax.random.fold_in(base_key, 3)
    groups = N_ROW * N_COL
    tile = M // groups
    values = jax.random.normal(value_key, (M, M), jnp.float32)
    values = (values + values.T) * 0.70710678
    pairing = jax.random.permutation(pair_key, groups)
    marks = jnp.zeros((groups, groups), jnp.float32).at[jnp.arange(groups), pairing].set(1.0)
    marks = jnp.maximum(marks, marks.T)
    factor = 1.0 + 3.0 * marks
    values = (values.reshape(groups, tile, groups, tile) * factor[:, None, :, None]).reshape(M, M)
    values = jnp.clip(values, -16.0, 16.0)
    return (values * M ** (-0.5)).astype(jnp.float32)


def block_levels(rng, extent, split, smallest, largest):
    loudness = 1.0
    for position, blocks in split:
        heights = jax.random.uniform(jax.random.fold_in(jax.random.fold_in(rng, 6), position), (blocks,), jnp.float32, smallest / len(split), largest / len(split))
        loudness = loudness * jnp.repeat(jnp.exp(heights), extent[position] // blocks).reshape((-1,) + (1,) * (len(extent) - 1 - position))
    return loudness


def normal_values(key, extent, deviation, bound, pieces=(), held_as=jnp.bfloat16):
    result = deviation * jax.random.normal(key, extent, jnp.float32)
    if pieces:
        result = result * block_levels(key, extent, pieces, -0.22, 0.18)
    return jnp.clip(result, -bound, bound).astype(held_as)


def setup_inputs(seed: int = 0) -> dict:
    arg_keys = jax.random.split(jax.random.key(seed), 9)
    return {
        "inverse_block": draw_inverse_block(jax.random.fold_in(arg_keys[8], 71), 0),
        "grid_position": jax.random.permutation(arg_keys[1], M).astype(jnp.int32),
        "panel_a": normal_values(arg_keys[2], (W, M), 0.25, 1.5, ((0, 8), (1, 16)), jnp.float32),
        "pivot_inverse_a": normal_values(arg_keys[3], (W, W), 1.0, 6.0, (), jnp.float32),
        "chosen_rows": draw_chosen_rows(jax.random.fold_in(arg_keys[8], 71), 0),
        "top_panel_b": normal_values(arg_keys[5], (W, W), 0.25, 1.5, (), jnp.float32),
        "panel_b": normal_values(arg_keys[6], (W, MB), 0.25, 1.5, ((0, 8), (1, 16)), jnp.float32),
        "pivot_inverse_b": normal_values(arg_keys[7], (W, W), 1.0, 6.0, (), jnp.float32),
    }


def spread(panel_t, positions, order):
    return jnp.zeros((order, panel_t.shape[0]), jnp.float32).at[positions].set(panel_t.T)


def reference(inverse_block, grid_position, panel_a, pivot_inverse_a, chosen_rows, top_panel_b, panel_b, pivot_inverse_b):
    exact = lax.Precision.HIGHEST
    order = inverse_block.shape[0]
    full_a = spread(panel_a, grid_position, order)
    inverse_panel_a = -jnp.dot(inverse_block, full_a, precision=exact, preferred_element_type=jnp.float32)
    diagonal_a = pivot_inverse_a - jnp.dot(full_a.T, inverse_panel_a, precision=exact, preferred_element_type=jnp.float32)
    positions_b = grid_position[chosen_rows]
    full_b = spread(panel_b, positions_b, order)
    selected = jnp.zeros((order,), jnp.float32).at[positions_b].set(1.0)
    cross = jnp.dot(inverse_panel_a.T, full_b, precision=exact, preferred_element_type=jnp.float32)
    inverse_top_b = -(jnp.dot(diagonal_a, top_panel_b, precision=exact, preferred_element_type=jnp.float32) + cross)
    bottom = jnp.dot(inverse_block, full_b, precision=exact, preferred_element_type=jnp.float32)
    bottom = bottom + jnp.dot(inverse_panel_a, top_panel_b, precision=exact, preferred_element_type=jnp.float32)
    inverse_panel_b = -bottom * selected[:, None]
    diagonal_b = pivot_inverse_b - jnp.dot(top_panel_b.T, inverse_top_b, precision=exact, preferred_element_type=jnp.float32)
    diagonal_b = diagonal_b - jnp.dot(full_b.T, inverse_panel_b, precision=exact, preferred_element_type=jnp.float32)
    return inverse_panel_a, diagonal_a, inverse_panel_b, inverse_top_b, diagonal_b
```

```python
import functools

import jax
import jax.numpy as jnp
from jax import lax
from jax.experimental import pallas as pl
from jax.experimental.pallas import tpu as pltpu
from jax.sharding import PartitionSpec as P

MESH = pl.DeviceIdType.MESH
F32 = jnp.float32
BF16 = jnp.bfloat16
NT = (((1,), (1,)), ((), ()))
W = 512
FEAT = 64
MA = 768
MB = 512
OWN = 96
COL_STEPS = ((0, 1), (0, 3), (0, 2), (1, 0), (1, 1), (1, 3), (1, 2))
ROW_STEPS = ((1, 0), (0, 1), (0, 3), (0, 2), (1, 1), (1, 3), (1, 2))


def split(x):
    high = x.astype(BF16)
    return high, (x - high.astype(F32)).astype(BF16)


def dot_nn(a, b):
    return jnp.dot(a, b, preferred_element_type=F32)


def dot_nt(a, b):
    return lax.dot_general(a, b, NT, preferred_element_type=F32)


def dot3(a, b):
    ah, al = split(a)
    bh, bl = split(b)
    return dot_nn(ah, bh) + (dot_nn(ah, bl) + dot_nn(al, bh))


def remote(src, dst, send, recv, device):
    return pltpu.make_async_remote_copy(
        src_ref=src,
        dst_ref=dst,
        send_sem=send,
        recv_sem=recv,
        device_id=device,
        device_id_type=MESH,
    )


def main_kernel(
    block_ref,
    gp_ref,
    gpt_ref,
    chosen_ref,
    pa_ref,
    pb_ref,
    out_pa_ref,
    out_pb_ref,
    out_sel_ref,
    out_g_ref,
    b_f32,
    b_high,
    b_low,
    gb,
    xa,
    xb,
    near,
    far,
    far_in,
    full,
    full_high,
    full_low,
    half_out,
    half_in,
    half_own,
    ring_in,
    own_out,
    own_in,
    gram,
    gram_core,
    gram_1,
    gram_2,
    gram_3,
    b_sem,
    y_send,
    y_recv,
    c_send,
    c_recv,
    far_send,
    far_recv,
    row_send,
    row_recv,
    half_send,
    half_recv,
    ring_send,
    ring_recv,
    own_send,
    own_recv,
    gc_send,
    gc_recv,
    gs_send,
    gs_recv,
    gg_send,
    gg_recv,
):
    r = lax.axis_index("row")
    c = lax.axis_index("col")
    x_lo, z = r // 4, r % 4
    x_hi, y, core = c // 8, (c // 2) % 4, c % 2
    x = x_hi * 2 + x_lo
    mate = (r, c + 1 - 2 * core)

    def col_device(dx, dy):
        return (r, (((x_hi + dx) % 2) * 4 + (y + dy) % 4) * 2 + core)

    def row_device(dx, dz):
        return (((x_lo + dx) % 2) * 4 + (z + dz) % 4, c)

    def x_device(dx):
        nx = (x + dx) % 4
        return ((nx % 2) * 4 + z, ((nx // 2) * 4 + y) * 2 + core)

    def y_device(dy):
        return col_device(0, dy)

    def z_device(dz):
        return row_device(0, dz)

    own_to = (c // 2, (c % 2) * 8 + r)
    own_from = (c % 8, 2 * r + c // 8)
    own_self = jnp.logical_and(own_to[0] == r, own_to[1] == c)

    block_copy = pltpu.make_async_copy(block_ref, b_f32, b_sem)
    block_copy.start()

    barrier = pltpu.get_barrier_semaphore()

    def greet(device):
        pl.semaphore_signal(barrier, inc=1, device_id=device, device_id_type=MESH)

    greet(mate)
    for dx, dy in COL_STEPS:
        greet(col_device(dx, (4 - dy) % 4))
    for dx, dz in ROW_STEPS:
        greet(row_device(dx, (4 - dz) % 4))
    for step in (1, 3):
        greet(x_device(4 - step))

    @pl.when(jnp.logical_not(own_self))
    def _():
        greet(own_from)
        pl.semaphore_wait(barrier, 18)

    @pl.when(own_self)
    def _():
        pl.semaphore_wait(barrier, 17)

    mine = y * 2 + core
    y_copies = []
    for i, dy in enumerate((1, 3, 2)):
        dev = y_device(dy)
        y_copies.append(
            (
                remote(pa_ref, xa.at[mine], y_send.at[0, i], y_recv.at[0, i], dev),
                remote(pb_ref, xb.at[mine], y_send.at[1, i], y_recv.at[1, i], dev),
            )
        )
    mate_copies = [
        (
            remote(pa_ref, xa.at[mine], c_send.at[0, 0], c_recv.at[0, 0], mate),
            remote(pb_ref, xb.at[mine], c_send.at[1, 0], c_recv.at[1, 0], mate),
        )
    ]
    for pair in mate_copies:
        for copy in pair:
            copy.start()
    for ab in range(2):
        for pair in y_copies:
            pair[ab].start()

    gpt = gpt_ref[...]
    table = jnp.concatenate([gpt >> 7, gpt & 127], axis=0).astype(F32).astype(BF16)
    own_start = r * (OWN * 16) + c * OWN
    tile = 1024

    def place(t, hits):
        ch = chosen_ref[:, pl.ds(pl.multiple_of(t * tile, tile), tile)]
        pick = jnp.where(
            lax.broadcasted_iota(jnp.int32, (96, tile), 0) == (ch >> 7), 1.0, 0.0
        ).astype(BF16)
        found = dot_nn(table, pick)
        value = found[:128] * 128.0 + found[128:]
        value = jnp.where(
            lax.broadcasted_iota(jnp.int32, (128, tile), 0) == (ch & 127), value, 0.0
        )
        position = jnp.sum(value, axis=0, keepdims=True).astype(jnp.int32)
        gb[:, pl.ds(pl.multiple_of(t * tile, tile), tile)] = position
        same = lax.broadcasted_iota(jnp.int32, (OWN, tile), 0) + own_start == position
        same = jnp.where(same, 1.0, 0.0)
        for i in range(tile // 128):
            hits = hits + same[:, i * 128 : (i + 1) * 128]
        return hits

    hits = lax.fori_loop(0, 8192 // tile, place, jnp.zeros((OWN, 128), F32))
    out_sel_ref[...] = jnp.broadcast_to(jnp.sum(hits, axis=1, keepdims=True), (OWN, 128))

    block_copy.wait()

    def divide(i, carry):
        rows = b_f32[pl.ds(pl.multiple_of(i * OWN, OWN), OWN), :]
        high, low = split(rows)
        b_high[i % 2, pl.ds(pl.multiple_of((i // 2) * OWN, OWN), OWN), :] = high
        b_low[i % 2, pl.ds(pl.multiple_of((i // 2) * OWN, OWN), OWN), :] = low
        return carry

    lax.fori_loop(0, 16, divide, 0)

    def take(panel, positions, first):
        width = panel.shape[1]
        hit = lax.broadcasted_iota(jnp.int32, (MA, width), 0) + first == positions
        hot = jnp.where(hit, 1.0, 0.0).astype(BF16)
        high, low = split(panel)
        both = dot_nt(jnp.concatenate([high, low], axis=0), hot)
        return both[:FEAT] + both[FEAT:]

    def gather(slot, target, to_x):
        first = ((to_x * 4 + y) * 2 + core) * MA
        source = x_hi * 8 + slot
        pos_a = gp_ref[:, pl.ds(pl.multiple_of(source * MA, 128), MA)]
        pos_b = gb[:, pl.ds(pl.multiple_of(source * MB, 128), MB)]
        target[:FEAT, :] += take(xa[slot], pos_a, first)
        target[FEAT:, :] += take(xb[slot], pos_b, first)

    xa[mine] = pa_ref[...]
    xb[mine] = pb_ref[...]
    near[...] = jnp.zeros_like(near)
    far[...] = jnp.zeros_like(far)
    gather(mine, far, 1 - x_hi)
    for copy in mate_copies[0]:
        copy.wait()
    gather(y * 2 + 1 - core, far, 1 - x_hi)
    for i, dy in enumerate((1, 3, 2)):
        from_slot = ((y + 4 - dy) % 4) * 2 + core
        pair = []
        for ab, buf in enumerate((xa, xb)):
            y_copies[i][ab].wait_recv()
            copy = remote(
                buf.at[from_slot],
                buf.at[from_slot],
                c_send.at[ab, i + 1],
                c_recv.at[ab, i + 1],
                mate,
            )
            copy.start()
            pair.append(copy)
        mate_copies.append(pair)
        gather(from_slot, far, 1 - x_hi)
        for copy in pair:
            copy.wait_recv()
        gather(((y + 4 - dy) % 4) * 2 + 1 - core, far, 1 - x_hi)
    far_copy = remote(far, far_in, far_send, far_recv, col_device(1, 0))
    far_copy.start()

    def gather_near(i, carry):
        gather(i, near, x_hi)
        return carry

    lax.fori_loop(0, 8, gather_near, 0)
    far_copy.wait()
    near[...] += far_in[...]
    for i in range(3):
        for ab in range(2):
            y_copies[i][ab].wait_send()
            mate_copies[i + 1][ab].wait_send()

    row_copies = []
    for ab in range(2):
        mine_f = near.at[pl.ds(ab * FEAT, FEAT), :]
        for i, (dx, dz) in enumerate(ROW_STEPS):
            copy = remote(
                mine_f,
                full.at[ab, r],
                row_send.at[ab, i],
                row_recv.at[ab, i],
                row_device(dx, dz),
            )
            copy.start()
            row_copies.append(copy)

    def store_full(ab, slot, value):
        high, low = split(value)
        full_high[ab, pl.ds(pl.multiple_of(slot * FEAT, FEAT), FEAT), :] = high
        full_low[ab, pl.ds(pl.multiple_of(slot * FEAT, FEAT), FEAT), :] = low

    for ab in range(2):
        store_full(ab, r, near[ab * FEAT : (ab + 1) * FEAT, :])

    def multiply(ab, part, target):
        def step(i, carry):
            rows = pl.ds(pl.multiple_of(i * 384, 384), 384)
            bh = b_high[part, rows, :]
            bl = b_low[part, rows, :]
            fh = full_high[ab]
            fl = full_low[ab]
            target[ab, rows, :] = dot_nt(bh, fh) + (dot_nt(bh, fl) + dot_nt(bl, fh))
            return carry

        lax.fori_loop(0, 2, step, 0)

    half_copies = []
    ring_copies = []
    for ab in range(2):
        for i, (dx, dz) in enumerate(ROW_STEPS):
            row_copies[ab * 7 + i].wait_recv()
            slot = ((x_lo + dx) % 2) * 4 + (z + 4 - dz) % 4
            store_full(ab, slot, full[ab, slot])
        multiply(ab, 1 - core, half_out)
        copy = remote(half_out.at[ab], half_in.at[ab], half_send.at[ab], half_recv.at[ab], mate)
        copy.start()
        half_copies.append(copy)
        multiply(ab, core, half_own)
        copy.wait_recv()
        half_own[ab] += half_in[ab]
        for i, (dx, dy) in enumerate(COL_STEPS):
            there = ((x_hi + dx) % 2) * 4 + (y + dy) % 4
            copy = remote(
                half_own.at[ab, pl.ds(pl.multiple_of(there * OWN, OWN), OWN), :],
                ring_in.at[ab, i],
                ring_send.at[ab, i],
                ring_recv.at[ab, i],
                col_device(dx, dy),
            )
            copy.start()
            ring_copies.append(copy)
    for copy in row_copies:
        copy.wait_send()

    pick = jnp.where(
        jnp.logical_and(
            lax.broadcasted_iota(jnp.int32, (128, MA), 0) + r * OWN
            == lax.broadcasted_iota(jnp.int32, (128, MA), 1),
            lax.broadcasted_iota(jnp.int32, (128, MA), 0) < OWN,
        ),
        1.0,
        0.0,
    ).astype(BF16)
    for ab in range(2):
        own_out[pl.ds(ab * W, W), :] = dot_nt(full_high[ab], pick) + dot_nt(full_low[ab], pick)
    own_copy = remote(own_out, own_in, own_send, own_recv, own_to)

    @pl.when(jnp.logical_not(own_self))
    def _():
        own_copy.start()

    @pl.when(own_self)
    def _():
        own_in[...] = own_out[...]

    here = pl.ds(pl.multiple_of((x_hi * 4 + y) * OWN, OWN), OWN)
    outs = (out_pa_ref, out_pb_ref)
    for ab in range(2):
        half_copies[ab].wait_send()
        total = half_own[ab, here, :]
        for i in range(7):
            ring_copies[ab * 7 + i].wait_recv()
            total = total + ring_in[ab, i]
        outs[ab][...] = total
    for copy in ring_copies:
        copy.wait_send()

    @pl.when(jnp.logical_not(own_self))
    def _():
        own_copy.wait()

    pad = jnp.zeros((128 - OWN, W), F32)
    ph_a, pl_a = split(jnp.concatenate([out_pa_ref[...], pad], axis=0))
    ph_b, pl_b = split(jnp.concatenate([out_pb_ref[...], pad], axis=0))
    fh_a, fl_a = split(own_in[:W, :])
    fh_b, fl_b = split(own_in[W:, :])

    def gram_of(fh, fl, ph, plow):
        return dot_nn(fh, ph) + (dot_nn(fh, plow) + dot_nn(fl, ph))

    gram[0:W, :] = gram_of(fh_a, fl_a, ph_a, pl_a)
    gram[W : 2 * W, :] = gram_of(fh_a, fl_a, ph_b, pl_b)
    gram[2 * W : 3 * W, :] = gram_of(fh_b, fl_b, ph_b, pl_b)
    half = 3 * W // 2
    copy = remote(
        gram.at[pl.ds(pl.multiple_of((1 - core) * half, half), half), :],
        gram_core,
        gc_send.at[0],
        gc_recv.at[0],
        mate,
    )
    copy.start()
    copy.wait()
    gram_core[...] += gram[pl.ds(pl.multiple_of(core * half, half), half), :]

    dims = ((x, x_device), (y, y_device), (z, z_device))
    orders = ((0, 1, 2), (1, 2, 0), (2, 0, 1))
    levels = []
    for p, order in enumerate(orders):
        q = [dims[d][0] for d in order]
        levels.append(
            (
                pl.multiple_of(p * 256, 256),
                q,
                [dims[d][1] for d in order],
            )
        )
    copies = []
    for p, (base, q, dev) in enumerate(levels):
        for i, step in enumerate((1, 3, 2)):
            to = (q[0] + step) % 4
            copy = remote(
                gram_core.at[pl.ds(pl.multiple_of(base + to * 64, 64), 64), :],
                gram_1.at[p, i],
                gs_send.at[0, p, i],
                gs_recv.at[0, p, i],
                dev[0](step),
            )
            copy.start()
            copies.append(copy)
    for p, (base, q, dev) in enumerate(levels):
        rows = pl.ds(pl.multiple_of(base + q[0] * 64, 64), 64)
        for i in range(3):
            copies[p * 3 + i].wait()
        gram_core[rows, :] += gram_1[p, 0] + gram_1[p, 1] + gram_1[p, 2]
        for i, step in enumerate((1, 3, 2)):
            to = (q[1] + step) % 4
            copy = remote(
                gram_core.at[pl.ds(pl.multiple_of(base + q[0] * 64 + to * 16, 16), 16), :],
                gram_2.at[p, i],
                gs_send.at[1, p, i],
                gs_recv.at[1, p, i],
                dev[1](step),
            )
            copy.start()
            copies.append(copy)
    for p, (base, q, dev) in enumerate(levels):
        rows = pl.ds(pl.multiple_of(base + q[0] * 64 + q[1] * 16, 16), 16)
        for i in range(3):
            copies[9 + p * 3 + i].wait()
        gram_core[rows, :] += gram_2[p, 0] + gram_2[p, 1] + gram_2[p, 2]
        for i, step in enumerate((1, 3, 2)):
            to = (q[2] + step) % 4
            copy = remote(
                gram_core.at[rows, pl.ds(pl.multiple_of(to * 128, 128), 128)],
                gram_3.at[p, i],
                gs_send.at[2, p, i],
                gs_recv.at[2, p, i],
                dev[2](step),
            )
            copy.start()
            copies.append(copy)
    home = core * half
    back = []

    def spread(level, p, ref, device):
        for i, step in enumerate((1, 3, 2)):
            copy = remote(
                ref, ref, gg_send.at[level, p, i], gg_recv.at[level, p, i], device(step)
            )
            copy.start()
            back.append(copy)

    for p, (base, q, dev) in enumerate(levels):
        row = base + q[0] * 64 + q[1] * 16
        column = pl.ds(pl.multiple_of(q[2] * 128, 128), 128)
        for i in range(3):
            copies[18 + p * 3 + i].wait()
        out_g_ref[pl.ds(pl.multiple_of(home + row, 16), 16), column] = (
            gram_core[pl.ds(pl.multiple_of(row, 16), 16), column]
            + gram_3[p, 0]
            + gram_3[p, 1]
            + gram_3[p, 2]
        )
        spread(0, p, out_g_ref.at[pl.ds(pl.multiple_of(home + row, 16), 16), column], dev[2])
    for p, (base, q, dev) in enumerate(levels):
        for i in range(3):
            back[p * 3 + i].wait()
        row = home + base + q[0] * 64 + q[1] * 16
        spread(1, p, out_g_ref.at[pl.ds(pl.multiple_of(row, 16), 16), :], dev[1])
    for p, (base, q, dev) in enumerate(levels):
        for i in range(3):
            back[9 + p * 3 + i].wait()
        row = home + base + q[0] * 64
        spread(2, p, out_g_ref.at[pl.ds(pl.multiple_of(row, 64), 64), :], dev[0])
    last = []
    for p, (base, q, dev) in enumerate(levels):
        for i in range(3):
            back[18 + p * 3 + i].wait()
        part = out_g_ref.at[pl.ds(pl.multiple_of(home + base, 256), 256), :]
        copy = remote(part, part, gc_send.at[1 + p], gc_recv.at[1 + p], mate)
        copy.start()
        last.append(copy)
    for copy in last:
        copy.wait()


def final_kernel(
    pa_ref, pb_ref, sel_ref, g_ref, pivot_a_ref, top_ref, pivot_b_ref, ia_ref, da_ref, ib_ref, tb_ref, db_ref
):
    top = top_ref[...]
    product_a = pa_ref[...]
    ia_ref[...] = -product_a
    ib_ref[...] = -(pb_ref[...] - dot3(product_a, top)) * sel_ref[:, :1]
    diagonal_a = pivot_a_ref[...] + g_ref[:W, :]
    da_ref[...] = diagonal_a
    cross_neg = g_ref[W : 2 * W, :]
    top_b = cross_neg - dot3(diagonal_a, top)
    tb_ref[...] = top_b
    top_t = top.T
    db_ref[...] = (
        pivot_b_ref[...] - dot3(top_t, top_b) + (g_ref[2 * W :, :] - dot3(cross_neg.T, top))
    )


def body(
    inverse_block,
    grid_position,
    panel_a,
    pivot_inverse_a,
    chosen_rows,
    top_panel_b,
    panel_b,
    pivot_inverse_b,
):
    vmem = pl.BlockSpec(memory_space=pltpu.VMEM)
    dma = pltpu.SemaphoreType.DMA
    out = jax.ShapeDtypeStruct
    gp = grid_position.reshape(1, -1)
    gpt = grid_position.reshape(96, 128).T
    product_a, product_b, selected, gram = pl.pallas_call(
        main_kernel,
        out_shape=(
            out((OWN, W), F32),
            out((OWN, W), F32),
            out((OWN, 128), F32),
            out((3 * W, W), F32),
        ),
        in_specs=[pl.BlockSpec(memory_space=pl.ANY)] + [vmem] * 5,
        out_specs=(vmem,) * 4,
        scratch_shapes=[
            pltpu.VMEM((1536, MA), F32),
            pltpu.VMEM((2, 768, MA), BF16),
            pltpu.VMEM((2, 768, MA), BF16),
            pltpu.VMEM((1, 8192), jnp.int32),
            pltpu.VMEM((8, FEAT, MA), F32),
            pltpu.VMEM((8, FEAT, MB), F32),
            pltpu.VMEM((2 * FEAT, MA), F32),
            pltpu.VMEM((2 * FEAT, MA), F32),
            pltpu.VMEM((2 * FEAT, MA), F32),
            pltpu.VMEM((2, 8, FEAT, MA), F32),
            pltpu.VMEM((2, W, MA), BF16),
            pltpu.VMEM((2, W, MA), BF16),
            pltpu.VMEM((2, 768, W), F32),
            pltpu.VMEM((2, 768, W), F32),
            pltpu.VMEM((2, 768, W), F32),
            pltpu.VMEM((2, 7, OWN, W), F32),
            pltpu.VMEM((2 * W, 128), F32),
            pltpu.VMEM((2 * W, 128), F32),
            pltpu.VMEM((3 * W, W), F32),
            pltpu.VMEM((3 * W // 2, W), F32),
            pltpu.VMEM((3, 3, 64, W), F32),
            pltpu.VMEM((3, 3, 16, W), F32),
            pltpu.VMEM((3, 3, 16, 128), F32),
            dma,
            dma((2, 3)),
            dma((2, 3)),
            dma((2, 4)),
            dma((2, 4)),
            dma,
            dma,
            dma((2, 7)),
            dma((2, 7)),
            dma((2,)),
            dma((2,)),
            dma((2, 7)),
            dma((2, 7)),
            dma,
            dma,
            dma((4,)),
            dma((4,)),
            dma((3, 3, 3)),
            dma((3, 3, 3)),
            dma((3, 3, 3)),
            dma((3, 3, 3)),
        ],
        compiler_params=pltpu.CompilerParams(
            collective_id=0, has_side_effects=True, vmem_limit_bytes=60 << 20
        ),
        cost_estimate=pl.CostEstimate(
            flops=10_000_000_000, bytes_accessed=20_000_000, transcendentals=0
        ),
        name="exchange",
    )(inverse_block, gp, gpt, chosen_rows.reshape(1, -1), panel_a, panel_b)
    return pl.pallas_call(
        final_kernel,
        out_shape=(
            out((OWN, W), F32),
            out((W, W), F32),
            out((OWN, W), F32),
            out((W, W), F32),
            out((W, W), F32),
        ),
        in_specs=[vmem] * 7,
        out_specs=(vmem,) * 5,
        compiler_params=pltpu.CompilerParams(vmem_limit_bytes=48 << 20),
        name="finish",
    )(product_a, product_b, selected, gram, pivot_inverse_a, top_panel_b, pivot_inverse_b)


def solution(mesh):
    in_specs = (P("row", "col"), P(), P("row", "col"), P(), P(), P(), P("row", "col"), P())
    out_specs = (P(("row", "col"), None), P(), P(("row", "col"), None), P(), P())
    return jax.shard_map(body, mesh=mesh, in_specs=in_specs, out_specs=out_specs, check_vma=False)
```

```python
import functools

import jax
import jax.numpy as jnp
from jax import lax
from jax.experimental import pallas as pl
from jax.experimental.pallas import tpu as pltpu
from jax.sharding import PartitionSpec as P

MESH = pl.DeviceIdType.MESH
F32 = jnp.float32
BF16 = jnp.bfloat16
NT = (((1,), (1,)), ((), ()))
W = 512
FEAT = 64
MA = 768
MB = 512
OWN = 96


def split(x):
    high = x.astype(BF16)
    return high, (x - high.astype(F32)).astype(BF16)


def dot_nn(a, b):
    return jnp.dot(a, b, preferred_element_type=F32)


def dot_nt(a, b):
    return lax.dot_general(a, b, NT, preferred_element_type=F32)


def dot3(a, b):
    ah, al = split(a)
    bh, bl = split(b)
    return dot_nn(ah, bh) + (dot_nn(ah, bl) + dot_nn(al, bh))


def remote(src, dst, send, recv, device):
    return pltpu.make_async_remote_copy(
        src_ref=src,
        dst_ref=dst,
        send_sem=send,
        recv_sem=recv,
        device_id=device,
        device_id_type=MESH,
    )


def main_kernel(
    block_ref,
    gp_ref,
    gpt_ref,
    chosen_ref,
    pa_ref,
    pb_ref,
    out_pa_ref,
    out_pb_ref,
    out_sel_ref,
    out_g_ref,
    b_f32,
    b_high,
    b_low,
    gb,
    xa,
    xb,
    near,
    far,
    far_in,
    full,
    full_high,
    full_low,
    half_out,
    half_in,
    half_own,
    ring_2,
    ring_1,
    x_out,
    x_in,
    own_out,
    own_in,
    gram,
    gram_core,
    gram_1,
    gram_2,
    gram_3,
    b_sem,
    y_send,
    y_recv,
    c_send,
    c_recv,
    far_send,
    far_recv,
    row_send,
    row_recv,
    half_send,
    half_recv,
    ring_send,
    ring_recv,
    x_send,
    x_recv,
    own_send,
    own_recv,
    gc_send,
    gc_recv,
    gs_send,
    gs_recv,
    gg_send,
    gg_recv,
):
    r = lax.axis_index("row")
    c = lax.axis_index("col")
    x_lo, z = r // 4, r % 4
    x_hi, y, core = c // 8, (c // 2) % 4, c % 2
    x = x_hi * 2 + x_lo
    mate = (r, c + 1 - 2 * core)

    def x_device(dx):
        nx = (x + dx) % 4
        return ((nx % 2) * 4 + z, ((nx // 2) * 4 + y) * 2 + core)

    def y_device(dy):
        return (r, (x_hi * 4 + (y + dy) % 4) * 2 + core)

    def z_device(dz):
        return (x_lo * 4 + (z + dz) % 4, c)

    x_pair = ((1 - x_lo) * 4 + z, c)
    x_across = x_device(2)
    own_to = (c // 2, (c % 2) * 8 + r)
    own_from = (c % 8, 2 * r + c // 8)
    own_self = jnp.logical_and(own_to[0] == r, own_to[1] == c)
    pending = []

    def send(src, dst, send_sem, recv_sem, device):
        copy = remote(src, dst, send_sem, recv_sem, device)
        copy.start()
        pending.append(copy)
        return copy

    def rows_of(start, size):
        return pl.ds(pl.multiple_of(start, size), size)

    block_copy = pltpu.make_async_copy(block_ref, b_f32, b_sem)
    block_copy.start()

    barrier = pltpu.get_barrier_semaphore()

    def greet(device):
        pl.semaphore_signal(barrier, inc=1, device_id=device, device_id_type=MESH)

    greet(mate)
    for step in (1, 2, 3):
        greet(x_device(4 - step))
        greet(y_device(4 - step))
        greet(z_device(4 - step))

    @pl.when(jnp.logical_not(own_self))
    def _():
        greet(own_from)
        pl.semaphore_wait(barrier, 11)

    @pl.when(own_self)
    def _():
        pl.semaphore_wait(barrier, 10)

    mine = y * 2 + core
    steps = (1, 3, 2)
    panels = (pa_ref, pb_ref)
    held = (xa, xb)
    y_copies = []
    mate_copies = []
    for ab in range(2):
        mate_copies.append(
            [send(panels[ab], held[ab].at[mine], c_send.at[ab, 0], c_recv.at[ab, 0], mate)]
        )
        y_copies.append(
            [
                send(
                    panels[ab], held[ab].at[mine], y_send.at[ab, i], y_recv.at[ab, i], y_device(dy)
                )
                for i, dy in enumerate(steps)
            ]
        )

    def pass_on(ab, i):
        slot = ((y + 4 - steps[i]) % 4) * 2 + core
        y_copies[ab][i].wait_recv()
        ref = held[ab].at[slot]
        mate_copies[ab].append(send(ref, ref, c_send.at[ab, i + 1], c_recv.at[ab, i + 1], mate))

    block_copy.wait()

    def divide(i, carry):
        high, low = split(b_f32[rows_of(i * OWN, OWN), :])
        b_high[i % 2, rows_of((i // 2) * OWN, OWN), :] = high
        b_low[i % 2, rows_of((i // 2) * OWN, OWN), :] = low
        return carry

    lax.fori_loop(0, 16, divide, 0)

    gpt = gpt_ref[...]
    table = jnp.concatenate([gpt >> 7, gpt & 127], axis=0).astype(F32).astype(BF16)
    own_start = r * (OWN * 16) + c * OWN
    tile = 1024

    def place(t, hits):
        ch = chosen_ref[:, rows_of(t * tile, tile)]
        pick = jnp.where(
            lax.broadcasted_iota(jnp.int32, (96, tile), 0) == (ch >> 7), 1.0, 0.0
        ).astype(BF16)
        found = dot_nn(table, pick)
        value = found[:128] * 128.0 + found[128:]
        value = jnp.where(
            lax.broadcasted_iota(jnp.int32, (128, tile), 0) == (ch & 127), value, 0.0
        )
        position = jnp.sum(value, axis=0, keepdims=True).astype(jnp.int32)
        gb[:, rows_of(t * tile, tile)] = position
        same = lax.broadcasted_iota(jnp.int32, (OWN, tile), 0) + own_start == position
        same = jnp.where(same, 1.0, 0.0)
        for i in range(tile // 128):
            hits = hits + same[:, i * 128 : (i + 1) * 128]
        return hits

    def take(panel, positions, first):
        width = panel.shape[1]
        hit = lax.broadcasted_iota(jnp.int32, (MA, width), 0) + first == positions
        hot = jnp.where(hit, 1.0, 0.0).astype(BF16)
        high, low = split(panel)
        both = dot_nt(jnp.concatenate([high, low], axis=0), hot)
        return both[:FEAT] + both[FEAT:]

    def gather(ab, slot, target, to_x):
        first = ((to_x * 4 + y) * 2 + core) * MA
        source = x_hi * 8 + slot
        if ab == 0:
            positions = gp_ref[:, pl.ds(pl.multiple_of(source * MA, 128), MA)]
        else:
            positions = gb[:, pl.ds(pl.multiple_of(source * MB, 128), MB)]
        target[ab] += take(held[ab][slot], positions, first)

    xa[mine] = pa_ref[...]
    xb[mine] = pb_ref[...]
    near[...] = jnp.zeros_like(near)
    far[...] = jnp.zeros_like(far)

    def gather_far(ab):
        gather(ab, mine, far, 1 - x_hi)
        mate_copies[ab][0].wait_recv()
        gather(ab, y * 2 + 1 - core, far, 1 - x_hi)
        for i, dy in enumerate(steps):
            base = ((y + 4 - dy) % 4) * 2
            if ab == 0:
                pass_on(ab, i)
            gather(ab, base + core, far, 1 - x_hi)
            mate_copies[ab][i + 1].wait_recv()
            gather(ab, base + 1 - core, far, 1 - x_hi)
        return send(far.at[ab], far_in.at[ab], far_send.at[ab], far_recv.at[ab], x_across)

    def gather_near(ab):
        def step(i, carry):
            gather(ab, i, near, x_hi)
            return carry

        lax.fori_loop(0, 8, step, 0)

    def store_full(ab, slot, value):
        high, low = split(value)
        full_high[ab, rows_of(slot * FEAT, FEAT), :] = high
        full_low[ab, rows_of(slot * FEAT, FEAT), :] = low

    row_copies = [{}, {}]
    sets = (x_lo, 1 - x_lo)

    def row_put(ab, name, src, slot, part, k, device):
        dst = full.at[ab, slot]
        if part is not None:
            dst = dst.at[pl.ds(part * 32, 32), :]
        row_copies[ab][name] = send(
            dst if src is None else src, dst, row_send.at[ab, k], row_recv.at[ab, k], device
        )

    def row_start(ab):
        src = near.at[ab]
        row_put(ab, "pair", src, r, None, 0, x_pair)
        row_put(ab, "up0", src, r, None, 1, z_device(1))
        row_put(ab, "down0", src, r, None, 2, z_device(3))
        store_full(ab, r, near[ab])

    def row_turn(ab, s):
        base = sets[s] * 4
        below = base + (z + 3) % 4
        above = base + (z + 1) % 4
        row_copies[ab]["up%d" % s].wait_recv()
        row_put(ab, "far_up%d" % s, None, below, 0, 3 + 4 * s, z_device(1))
        row_copies[ab]["down%d" % s].wait_recv()
        row_put(ab, "far_down%d" % s, None, above, 1, 4 + 4 * s, z_device(3))
        if s == 0:
            other = (1 - x_lo) * 4 + z
            row_copies[ab]["pair"].wait_recv()
            row_put(ab, "up1", None, other, None, 5, z_device(1))
            row_put(ab, "down1", None, other, None, 6, z_device(3))
            store_full(ab, other, full[ab, other])
        store_full(ab, below, full[ab, below])
        store_full(ab, above, full[ab, above])

    def row_end(ab):
        for s in range(2):
            slot = sets[s] * 4 + (z + 2) % 4
            row_copies[ab]["far_up%d" % s].wait_recv()
            row_copies[ab]["far_down%d" % s].wait_recv()
            store_full(ab, slot, full[ab, slot])

    halves = (1 - x_hi, x_hi)

    def multiply(ab, part, half, target):
        rows = rows_of(half * 384, 384)
        bh = b_high[part, rows, :]
        bl = b_low[part, rows, :]
        fh = full_high[ab]
        fl = full_low[ab]
        target[ab, rows, :] = dot_nt(bh, fh) + (dot_nt(bh, fl) + dot_nt(bl, fh))

    half_copies = [[None, None], [None, None]]

    def product_out(ab, s):
        rows = rows_of(halves[s] * 384, 384)
        multiply(ab, 1 - core, halves[s], half_out)
        half_copies[ab][s] = send(
            half_out.at[ab, rows, :],
            half_in.at[ab, rows, :],
            half_send.at[ab, s],
            half_recv.at[ab, s],
            mate,
        )

    def product_own(ab, s):
        rows = rows_of(halves[s] * 384, 384)
        multiply(ab, core, halves[s], half_own)
        half_copies[ab][s].wait_recv()
        half_own[ab, rows, :] += half_in[ab, rows, :]

    ring_copies = {}

    def chunk(s, dy, part=None):
        start = (halves[s] * 4 + (y + dy) % 4) * OWN
        if part is None:
            return rows_of(start, OWN)
        return rows_of(start + part * 48, 48)

    def ring_put(ab, s, name, k, src_rows, dst, device):
        ring_copies[ab, s, name] = send(
            half_own.at[ab, src_rows, :], dst, ring_send.at[ab, s, k], ring_recv.at[ab, s, k], device
        )

    low_part = pl.ds(0, 48)
    high_part = pl.ds(48, 48)

    def ring_start(ab, s):
        up, down = y_device(1), y_device(3)
        ring_put(ab, s, "two_up", 0, chunk(s, 2, 0), ring_2.at[ab, s, 0], up)
        ring_put(ab, s, "two_down", 1, chunk(s, 2, 1), ring_2.at[ab, s, 1], down)
        ring_put(ab, s, "up_high", 2, chunk(s, 1, 1), ring_1.at[ab, s, 0, high_part, :], up)
        ring_put(ab, s, "down_low", 3, chunk(s, 3, 0), ring_1.at[ab, s, 1, low_part, :], down)

    def ring_turn(ab, s):
        up, down = y_device(1), y_device(3)
        ring_copies[ab, s, "two_up"].wait_recv()
        half_own[ab, chunk(s, 1, 0), :] += ring_2[ab, s, 0]
        ring_put(ab, s, "up_low", 4, chunk(s, 1, 0), ring_1.at[ab, s, 0, low_part, :], up)
        ring_copies[ab, s, "two_down"].wait_recv()
        half_own[ab, chunk(s, 3, 1), :] += ring_2[ab, s, 1]
        ring_put(ab, s, "down_high", 5, chunk(s, 3, 1), ring_1.at[ab, s, 1, high_part, :], down)

    def ring_sum(ab, s):
        for name in ("up_high", "down_low", "up_low", "down_high"):
            ring_copies[ab, s, name].wait_recv()
        return half_own[ab, chunk(s, 0), :] + ring_1[ab, s, 0] + ring_1[ab, s, 1]

    def ring_across(ab):
        x_out[ab] = ring_sum(ab, 0)
        ring_copies[ab] = send(
            x_out.at[ab], x_in.at[ab], x_send.at[ab], x_recv.at[ab], x_across
        )

    def ring_end(ab):
        total = ring_sum(ab, 1)
        ring_copies[ab].wait_recv()
        total = total + x_in[ab]
        (out_pa_ref, out_pb_ref)[ab][...] = total
        return total

    own_copies = []

    def own_start_copy(ab):
        line = lax.broadcasted_iota(jnp.int32, (128, MA), 0)
        pick = jnp.where(
            jnp.logical_and(
                line + r * OWN == lax.broadcasted_iota(jnp.int32, (128, MA), 1), line < OWN
            ),
            1.0,
            0.0,
        ).astype(BF16)
        own_out[ab] = dot_nt(full_high[ab], pick) + dot_nt(full_low[ab], pick)
        copy = remote(own_out.at[ab], own_in.at[ab], own_send.at[ab], own_recv.at[ab], own_to)
        own_copies.append(copy)

        @pl.when(jnp.logical_not(own_self))
        def _():
            copy.start()

        @pl.when(own_self)
        def _():
            own_in[ab] = own_out[ab]

    def own_wait(ab):
        @pl.when(jnp.logical_not(own_self))
        def _():
            own_copies[ab].wait()

    dims = ((x, x_device), (y, y_device), (z, z_device))
    parts = []
    for where, size, home, order in (
        (0, 256, core * 512, (0, 1, 2)),
        (256, 256, core * 512 + 256, (1, 2, 0)),
        (512, 128, 1024 + core * 256, (2, 0, 1)),
        (640, 128, 1024 + core * 256 + 128, (1, 2, 0)),
    ):
        q = [dims[d][0] for d in order]
        parts.append((where, size, home, q, [dims[d][1] for d in order]))
    gram_copies = {}

    def gram_step(p, n):
        where, size, home, q, dev = parts[p]
        one, two = size // 4, size // 16
        row_1 = q[0] * one
        row_2 = row_1 + q[1] * two
        column = pl.ds(pl.multiple_of(q[2] * 128, 128), 128)
        if n > 0:
            for copy in gram_copies[p, n - 1]:
                copy.wait_recv()
        copies = []
        gram_copies[p, n] = copies
        if n == 0:
            pass
        elif n == 1:
            rows = rows_of(where + row_1, one)
            got = [gram_1[p, i, 0:one, :] for i in range(3)]
            gram_core[rows, :] += got[0] + got[1] + got[2]
        elif n == 2:
            rows = rows_of(where + row_2, two)
            got = [gram_2[p, i, 0:two, :] for i in range(3)]
            gram_core[rows, :] += got[0] + got[1] + got[2]
        elif n == 3:
            rows = rows_of(where + row_2, two)
            got = [gram_3[p, i, 0:two, :] for i in range(3)]
            out_g_ref[rows_of(home + row_2, two), column] = (
                gram_core[rows, column] + got[0] + got[1] + got[2]
            )
        for i, step in enumerate(steps):
            if n == 0:
                src = gram_core.at[rows_of(where + ((q[0] + step) % 4) * one, one), :]
                dst = gram_1.at[p, i, pl.ds(0, one), :]
            elif n == 1:
                src = gram_core.at[rows_of(where + row_1 + ((q[1] + step) % 4) * two, two), :]
                dst = gram_2.at[p, i, pl.ds(0, two), :]
            elif n == 2:
                to = pl.ds(pl.multiple_of(((q[2] + step) % 4) * 128, 128), 128)
                src = gram_core.at[rows_of(where + row_2, two), to]
                dst = gram_3.at[p, i, pl.ds(0, two), :]
            elif n == 3:
                src = dst = out_g_ref.at[rows_of(home + row_2, two), column]
            elif n == 4:
                src = dst = out_g_ref.at[rows_of(home + row_2, two), :]
            elif n == 5:
                src = dst = out_g_ref.at[rows_of(home + row_1, one), :]
            if n < 6:
                d = dev[n if n < 3 else 5 - n]
                copies.append(send(src, dst, gs_send.at[p, n, i], gs_recv.at[p, n, i], d(step)))
        if n == 6:
            src = dst = out_g_ref.at[rows_of(home, size), :]
            copies.append(send(src, dst, gg_send.at[p], gg_recv.at[p], mate))

    def gram_of(f, p):
        fh, fl = split(f)
        ph, low = split(jnp.concatenate([p, jnp.zeros((128 - OWN, W), F32)], axis=0))
        return dot_nn(fh, ph) + (dot_nn(fh, low) + dot_nn(fl, ph))

    hits = lax.fori_loop(0, 8192 // tile, place, jnp.zeros((OWN, 128), F32))
    out_sel_ref[...] = jnp.broadcast_to(jnp.sum(hits, axis=1, keepdims=True), (OWN, 128))
    far_a = gather_far(0)
    gather_near(0)
    for i in range(3):
        pass_on(1, i)
    far_a.wait_recv()
    near[0] += far_in[0]
    row_start(0)
    far_b = gather_far(1)
    row_turn(0, 0)
    gather_near(1)
    far_b.wait_recv()
    near[1] += far_in[1]
    row_start(1)
    row_turn(0, 1)
    row_turn(1, 0)
    row_end(0)
    product_out(0, 0)
    product_out(0, 1)
    product_own(0, 0)
    ring_start(0, 0)
    product_own(0, 1)
    ring_start(0, 1)
    row_turn(1, 1)
    own_start_copy(0)
    ring_turn(0, 0)
    ring_turn(0, 1)
    row_end(1)
    product_out(1, 0)
    product_out(1, 1)
    ring_across(0)
    product_own(1, 0)
    ring_start(1, 0)
    product_own(1, 1)
    ring_start(1, 1)
    own_start_copy(1)
    product_a = ring_end(0)
    ring_turn(1, 0)
    ring_turn(1, 1)
    own_wait(0)
    gram[0:W, :] = gram_of(own_in[0], product_a)
    own_wait(1)
    gram[W : 2 * W, :] = gram_of(own_in[1], product_a)
    core_a = send(
        gram.at[rows_of((1 - core) * W, W), :],
        gram_core.at[0:W, :],
        gc_send.at[0],
        gc_recv.at[0],
        mate,
    )
    core_a.wait_recv()
    gram_core[0:W, :] += gram[rows_of(core * W, W), :]
    gram_step(0, 0)
    gram_step(1, 0)
    ring_across(1)
    gram_step(0, 1)
    gram_step(1, 1)
    product_b = ring_end(1)
    gram[2 * W : 3 * W, :] = gram_of(own_in[1], product_b)
    core_b = send(
        gram.at[rows_of(2 * W + (1 - core) * 256, 256), :],
        gram_core.at[W : W + 256, :],
        gc_send.at[1],
        gc_recv.at[1],
        mate,
    )
    gram_step(0, 2)
    gram_step(1, 2)
    core_b.wait_recv()
    gram_core[W : W + 256, :] += gram[rows_of(2 * W + core * 256, 256), :]
    gram_step(2, 0)
    gram_step(3, 0)
    gram_step(0, 3)
    gram_step(1, 3)
    for n in range(1, 7):
        gram_step(2, n)
        gram_step(3, n)
        if n + 3 < 7:
            gram_step(0, n + 3)
            gram_step(1, n + 3)
    for p in range(4):
        gram_copies[p, 6][0].wait_recv()
    for copy in pending:
        copy.wait_send()


def final_kernel(
    pa_ref, pb_ref, sel_ref, g_ref, pivot_a_ref, top_ref, pivot_b_ref, ia_ref, da_ref, ib_ref, tb_ref, db_ref
):
    top = top_ref[...]
    product_a = pa_ref[...]
    ia_ref[...] = -product_a
    ib_ref[...] = -(pb_ref[...] - dot3(product_a, top)) * sel_ref[:, :1]
    diagonal_a = pivot_a_ref[...] + g_ref[:W, :]
    da_ref[...] = diagonal_a
    cross_neg_t = g_ref[W : 2 * W, :]
    cross_neg = cross_neg_t.T
    top_b = cross_neg - dot3(diagonal_a, top)
    tb_ref[...] = top_b
    top_t = top.T
    db_ref[...] = (
        pivot_b_ref[...] - dot3(top_t, top_b) + (g_ref[2 * W :, :] - dot3(cross_neg_t, top))
    )


def body(
    inverse_block,
    grid_position,
    panel_a,
    pivot_inverse_a,
    chosen_rows,
    top_panel_b,
    panel_b,
    pivot_inverse_b,
):
    vmem = pl.BlockSpec(memory_space=pltpu.VMEM)
    dma = pltpu.SemaphoreType.DMA
    out = jax.ShapeDtypeStruct
    gp = grid_position.reshape(1, -1)
    gpt = grid_position.reshape(96, 128).T
    product_a, product_b, selected, gram = pl.pallas_call(
        main_kernel,
        out_shape=(
            out((OWN, W), F32),
            out((OWN, W), F32),
            out((OWN, 128), F32),
            out((3 * W, W), F32),
        ),
        in_specs=[pl.BlockSpec(memory_space=pl.ANY)] + [vmem] * 5,
        out_specs=(vmem,) * 4,
        scratch_shapes=[
            pltpu.VMEM((1536, MA), F32),
            pltpu.VMEM((2, 768, MA), BF16),
            pltpu.VMEM((2, 768, MA), BF16),
            pltpu.VMEM((1, 8192), jnp.int32),
            pltpu.VMEM((8, FEAT, MA), F32),
            pltpu.VMEM((8, FEAT, MB), F32),
            pltpu.VMEM((2, FEAT, MA), F32),
            pltpu.VMEM((2, FEAT, MA), F32),
            pltpu.VMEM((2, FEAT, MA), F32),
            pltpu.VMEM((2, 8, FEAT, MA), F32),
            pltpu.VMEM((2, W, MA), BF16),
            pltpu.VMEM((2, W, MA), BF16),
            pltpu.VMEM((2, 768, W), F32),
            pltpu.VMEM((2, 768, W), F32),
            pltpu.VMEM((2, 768, W), F32),
            pltpu.VMEM((2, 2, 2, 48, W), F32),
            pltpu.VMEM((2, 2, 2, OWN, W), F32),
            pltpu.VMEM((2, OWN, W), F32),
            pltpu.VMEM((2, OWN, W), F32),
            pltpu.VMEM((2, W, 128), F32),
            pltpu.VMEM((2, W, 128), F32),
            pltpu.VMEM((3 * W, W), F32),
            pltpu.VMEM((3 * W // 2, W), F32),
            pltpu.VMEM((4, 3, 64, W), F32),
            pltpu.VMEM((4, 3, 16, W), F32),
            pltpu.VMEM((4, 3, 16, 128), F32),
            dma,
            dma((2, 3)),
            dma((2, 3)),
            dma((2, 4)),
            dma((2, 4)),
            dma((2,)),
            dma((2,)),
            dma((2, 9)),
            dma((2, 9)),
            dma((2, 2)),
            dma((2, 2)),
            dma((2, 2, 6)),
            dma((2, 2, 6)),
            dma((2,)),
            dma((2,)),
            dma((2,)),
            dma((2,)),
            dma((2,)),
            dma((2,)),
            dma((4, 6, 3)),
            dma((4, 6, 3)),
            dma((4,)),
            dma((4,)),
        ],
        compiler_params=pltpu.CompilerParams(
            collective_id=0, has_side_effects=True, vmem_limit_bytes=60 << 20
        ),
        cost_estimate=pl.CostEstimate(
            flops=10_000_000_000, bytes_accessed=20_000_000, transcendentals=0
        ),
        name="exchange",
    )(inverse_block, gp, gpt, chosen_rows.reshape(1, -1), panel_a, panel_b)
    return pl.pallas_call(
        final_kernel,
        out_shape=(
            out((OWN, W), F32),
            out((W, W), F32),
            out((OWN, W), F32),
            out((W, W), F32),
            out((W, W), F32),
        ),
        in_specs=[vmem] * 7,
        out_specs=(vmem,) * 5,
        compiler_params=pltpu.CompilerParams(vmem_limit_bytes=48 << 20),
        name="finish",
    )(product_a, product_b, selected, gram, pivot_inverse_a, top_panel_b, pivot_inverse_b)


def solution(mesh):
    in_specs = (P("row", "col"), P(), P("row", "col"), P(), P(), P(), P("row", "col"), P())
    out_specs = (P(("row", "col"), None), P(), P(("row", "col"), None), P(), P())
    return jax.shard_map(body, mesh=mesh, in_specs=in_specs, out_specs=out_specs, check_vma=False)
```

```python
import functools

import jax
import jax.numpy as jnp
from jax import lax
from jax.experimental import pallas as pl
from jax.experimental.pallas import tpu as pltpu
from jax.sharding import PartitionSpec as P

MESH = pl.DeviceIdType.MESH
F32 = jnp.float32
BF16 = jnp.bfloat16
NT = (((1,), (1,)), ((), ()))
TN = (((0,), (0,)), ((), ()))
W = 512
FEAT = 64
MA = 768
MB = 512
OWN = 96


def split(x):
    high = x.astype(BF16)
    return high, (x - high.astype(F32)).astype(BF16)


def dot_nn(a, b):
    return jnp.dot(a, b, preferred_element_type=F32)


def dot_nt(a, b):
    return lax.dot_general(a, b, NT, preferred_element_type=F32)


def dot_tn(a, b):
    return lax.dot_general(a, b, TN, preferred_element_type=F32)


def dot3(a, b):
    ah, al = split(a)
    bh, bl = split(b)
    return dot_nn(ah, bh) + (dot_nn(ah, bl) + dot_nn(al, bh))


def remote(src, dst, send, recv, device):
    return pltpu.make_async_remote_copy(
        src_ref=src,
        dst_ref=dst,
        send_sem=send,
        recv_sem=recv,
        device_id=device,
        device_id_type=MESH,
    )


def main_kernel(
    block_ref,
    gp_ref,
    gpt_ref,
    chosen_ref,
    pa_ref,
    pb_ref,
    out_g_ref,
    b_f32,
    b_high,
    b_low,
    gb,
    xa,
    xb,
    near,
    far,
    far_in,
    full,
    full_high,
    full_low,
    half_out,
    half_in,
    half_own,
    ring_2,
    ring_1,
    x_out,
    x_in,
    own_out,
    own_in,
    gram,
    gram_core,
    gram_1,
    gram_2,
    gram_3,
    b_sem,
    y_send,
    y_recv,
    c_send,
    c_recv,
    far_send,
    far_recv,
    row_send,
    row_recv,
    half_send,
    half_recv,
    ring_send,
    ring_recv,
    x_send,
    x_recv,
    own_send,
    own_recv,
    gc_send,
    gc_recv,
    gs_send,
    gs_recv,
    gg_send,
    gg_recv,
):
    r = lax.axis_index("row")
    c = lax.axis_index("col")
    x_lo, z = r // 4, r % 4
    x_hi, y, core = c // 8, (c // 2) % 4, c % 2
    x = x_hi * 2 + x_lo
    mate = (r, c + 1 - 2 * core)

    def x_device(dx):
        nx = (x + dx) % 4
        return ((nx % 2) * 4 + z, ((nx // 2) * 4 + y) * 2 + core)

    def y_device(dy):
        return (r, (x_hi * 4 + (y + dy) % 4) * 2 + core)

    def z_device(dz):
        return (x_lo * 4 + (z + dz) % 4, c)

    x_pair = ((1 - x_lo) * 4 + z, c)
    x_across = x_device(2)
    own_part = ((y + z) % 4) * 2 + x_lo
    own_to = (c // 2, core * 8 + own_part)
    own_from = (core * 4 + (y + 4 - z) % 4, 2 * r + x_hi)
    own_self = jnp.logical_and(own_to[0] == r, own_to[1] == c)
    pending = []

    def send(src, dst, send_sem, recv_sem, device):
        copy = remote(src, dst, send_sem, recv_sem, device)
        copy.start()
        pending.append(copy)
        return copy

    def rows_of(start, size):
        return pl.ds(pl.multiple_of(start, size), size)

    block_copy = pltpu.make_async_copy(block_ref, b_f32, b_sem)
    block_copy.start()

    barrier = pltpu.get_barrier_semaphore()

    def greet(device):
        pl.semaphore_signal(barrier, inc=1, device_id=device, device_id_type=MESH)

    greet(mate)
    for step in (1, 2, 3):
        greet(x_device(4 - step))
        greet(y_device(4 - step))
        greet(z_device(4 - step))

    @pl.when(jnp.logical_not(own_self))
    def _():
        greet(own_from)
        pl.semaphore_wait(barrier, 11)

    @pl.when(own_self)
    def _():
        pl.semaphore_wait(barrier, 10)

    mine = y * 2 + core
    steps = (1, 3, 2)
    panels = (pa_ref, pb_ref)
    held = (xa, xb)
    y_copies = [None, None]
    mate_copies = [None, None]

    def y_start(ab):
        mate_copies[ab] = [
            send(panels[ab], held[ab].at[mine], c_send.at[ab, 0], c_recv.at[ab, 0], mate)
        ]
        y_copies[ab] = [
            send(panels[ab], held[ab].at[mine], y_send.at[ab, i], y_recv.at[ab, i], y_device(dy))
            for i, dy in enumerate(steps)
        ]

    y_start(0)

    def pass_on(ab, i):
        slot = ((y + 4 - steps[i]) % 4) * 2 + core
        y_copies[ab][i].wait_recv()
        ref = held[ab].at[slot]
        mate_copies[ab].append(send(ref, ref, c_send.at[ab, i + 1], c_recv.at[ab, i + 1], mate))

    block_copy.wait()

    def divide(i, carry):
        high, low = split(b_f32[rows_of(i * OWN, OWN), :])
        b_high[i % 2, rows_of((i // 2) * OWN, OWN), :] = high
        b_low[i % 2, rows_of((i // 2) * OWN, OWN), :] = low
        return carry

    lax.fori_loop(0, 16, divide, 0)

    gpt = gpt_ref[...]
    table = jnp.concatenate([gpt >> 7, gpt & 127], axis=1).astype(F32).T.astype(BF16)
    own_start = r * (OWN * 16) + c * OWN
    tile = 1024

    def place(t, hits):
        ch = chosen_ref[:, rows_of(t * tile, tile)]
        pick = jnp.where(
            lax.broadcasted_iota(jnp.int32, (96, tile), 0) == (ch >> 7), 1.0, 0.0
        ).astype(BF16)
        found = dot_nn(table, pick)
        value = found[:128] * 128.0 + found[128:]
        value = jnp.where(
            lax.broadcasted_iota(jnp.int32, (128, tile), 0) == (ch & 127), value, 0.0
        )
        position = jnp.sum(value, axis=0, keepdims=True).astype(jnp.int32)
        gb[:, rows_of(t * tile, tile)] = position
        same = lax.broadcasted_iota(jnp.int32, (OWN, tile), 0) + own_start == position
        same = jnp.where(same, 1.0, 0.0)
        for i in range(tile // 128):
            hits = hits + same[:, i * 128 : (i + 1) * 128]
        return hits

    def take(panel, positions, first):
        width = panel.shape[1]
        hit = lax.broadcasted_iota(jnp.int32, (MA, width), 0) + first == positions
        hot = jnp.where(hit, 1.0, 0.0).astype(BF16)
        high, low = split(panel)
        both = dot_nt(jnp.concatenate([high, low], axis=0), hot)
        return both[:FEAT] + both[FEAT:]

    def gather(ab, slot, target, to_x):
        first = ((to_x * 4 + y) * 2 + core) * MA
        source = x_hi * 8 + slot
        if ab == 0:
            positions = gp_ref[:, pl.ds(pl.multiple_of(source * MA, 128), MA)]
        else:
            positions = gb[:, pl.ds(pl.multiple_of(source * MB, 128), MB)]
        target[ab] += take(held[ab][slot], positions, first)

    xa[mine] = pa_ref[...]
    xb[mine] = pb_ref[...]
    near[...] = jnp.zeros_like(near)
    far[...] = jnp.zeros_like(far)

    def gather_far(ab):
        gather(ab, mine, far, 1 - x_hi)
        mate_copies[ab][0].wait_recv()
        gather(ab, y * 2 + 1 - core, far, 1 - x_hi)
        for i, dy in enumerate(steps):
            base = ((y + 4 - dy) % 4) * 2
            if ab == 0:
                pass_on(ab, i)
            gather(ab, base + core, far, 1 - x_hi)
            mate_copies[ab][i + 1].wait_recv()
            gather(ab, base + 1 - core, far, 1 - x_hi)
        return send(far.at[ab], far_in.at[ab], far_send.at[ab], far_recv.at[ab], x_across)

    def gather_near(ab):
        def step(i, carry):
            gather(ab, i, near, x_hi)
            return carry

        lax.fori_loop(0, 8, step, 0)

    def store_full(ab, slot, value):
        high, low = split(value)
        full_high[ab, rows_of(slot * FEAT, FEAT), :] = high
        full_low[ab, rows_of(slot * FEAT, FEAT), :] = low

    row_copies = [{}, {}]
    sets = (x_lo, 1 - x_lo)

    def row_put(ab, name, src, slot, part, k, device):
        dst = full.at[ab, slot]
        if part is not None:
            dst = dst.at[pl.ds(part * 32, 32), :]
        row_copies[ab][name] = send(
            dst if src is None else src, dst, row_send.at[ab, k], row_recv.at[ab, k], device
        )

    def row_start(ab):
        src = near.at[ab]
        row_put(ab, "pair", src, r, None, 0, x_pair)
        row_put(ab, "up0", src, r, None, 1, z_device(1))
        row_put(ab, "down0", src, r, None, 2, z_device(3))
        store_full(ab, r, near[ab])

    def row_turn(ab, s):
        base = sets[s] * 4
        below = base + (z + 3) % 4
        above = base + (z + 1) % 4
        row_copies[ab]["up%d" % s].wait_recv()
        row_put(ab, "far_up%d" % s, None, below, 0, 3 + 4 * s, z_device(1))
        row_copies[ab]["down%d" % s].wait_recv()
        row_put(ab, "far_down%d" % s, None, above, 1, 4 + 4 * s, z_device(3))
        if s == 0:
            other = (1 - x_lo) * 4 + z
            row_copies[ab]["pair"].wait_recv()
            row_put(ab, "up1", None, other, None, 5, z_device(1))
            row_put(ab, "down1", None, other, None, 6, z_device(3))
            store_full(ab, other, full[ab, other])
        store_full(ab, below, full[ab, below])
        store_full(ab, above, full[ab, above])

    def row_end(ab):
        for s in range(2):
            slot = sets[s] * 4 + (z + 2) % 4
            row_copies[ab]["far_up%d" % s].wait_recv()
            row_copies[ab]["far_down%d" % s].wait_recv()
            store_full(ab, slot, full[ab, slot])

    halves = (1 - x_hi, x_hi)

    def multiply(ab, part, half, target):
        rows = rows_of(half * 384, 384)
        bh = b_high[part, rows, :]
        bl = b_low[part, rows, :]
        fh = full_high[ab]
        fl = full_low[ab]
        target[ab, rows, :] = dot_nt(bh, fh) + (dot_nt(bh, fl) + dot_nt(bl, fh))

    half_copies = [[None, None], [None, None]]

    def product_out(ab, s):
        rows = rows_of(halves[s] * 384, 384)
        multiply(ab, 1 - core, halves[s], half_out)
        half_copies[ab][s] = send(
            half_out.at[ab, rows, :],
            half_in.at[ab, rows, :],
            half_send.at[ab, s],
            half_recv.at[ab, s],
            mate,
        )

    def product_own(ab, s):
        rows = rows_of(halves[s] * 384, 384)
        multiply(ab, core, halves[s], half_own)
        half_copies[ab][s].wait_recv()
        half_own[ab, rows, :] += half_in[ab, rows, :]

    ring_copies = {}

    def chunk(s, dy, part=None):
        start = (halves[s] * 4 + (y + dy) % 4) * OWN
        if part is None:
            return rows_of(start, OWN)
        return rows_of(start + part * 48, 48)

    def ring_put(ab, s, name, k, src_rows, dst, device):
        ring_copies[ab, s, name] = send(
            half_own.at[ab, src_rows, :], dst, ring_send.at[ab, s, k], ring_recv.at[ab, s, k], device
        )

    low_part = pl.ds(0, 48)
    high_part = pl.ds(48, 48)

    def ring_start(ab, s):
        up, down = y_device(1), y_device(3)
        ring_put(ab, s, "two_up", 0, chunk(s, 2, 0), ring_2.at[ab, s, 0], up)
        ring_put(ab, s, "two_down", 1, chunk(s, 2, 1), ring_2.at[ab, s, 1], down)
        ring_put(ab, s, "up_high", 2, chunk(s, 1, 1), ring_1.at[ab, s, 0, high_part, :], up)
        ring_put(ab, s, "down_low", 3, chunk(s, 3, 0), ring_1.at[ab, s, 1, low_part, :], down)

    def ring_turn(ab, s):
        up, down = y_device(1), y_device(3)
        ring_copies[ab, s, "two_up"].wait_recv()
        half_own[ab, chunk(s, 1, 0), :] += ring_2[ab, s, 0]
        ring_put(ab, s, "up_low", 4, chunk(s, 1, 0), ring_1.at[ab, s, 0, low_part, :], up)
        ring_copies[ab, s, "two_down"].wait_recv()
        half_own[ab, chunk(s, 3, 1), :] += ring_2[ab, s, 1]
        ring_put(ab, s, "down_high", 5, chunk(s, 3, 1), ring_1.at[ab, s, 1, high_part, :], down)

    def ring_sum(ab, s):
        for name in ("up_high", "down_low", "up_low", "down_high"):
            ring_copies[ab, s, name].wait_recv()
        return half_own[ab, chunk(s, 0), :] + ring_1[ab, s, 0] + ring_1[ab, s, 1]

    def ring_across(ab):
        x_out[ab] = ring_sum(ab, 0)
        ring_copies[ab] = send(
            x_out.at[ab], x_in.at[ab], x_send.at[ab], x_recv.at[ab], x_across
        )

    def ring_end(ab):
        total = ring_sum(ab, 1)
        ring_copies[ab].wait_recv()
        total = total + x_in[ab]
        out_g_ref[pl.ds(3 * W + ab * OWN, OWN), :] = total
        return total

    own_copies = []

    def own_start_copy(ab):
        line = lax.broadcasted_iota(jnp.int32, (OWN, MA), 0) + own_part * OWN
        pick = jnp.where(line == lax.broadcasted_iota(jnp.int32, (OWN, MA), 1), 1.0, 0.0)
        pick = pick.astype(BF16)
        own_out[ab] = dot_nt(pick, full_high[ab]) + dot_nt(pick, full_low[ab])
        copy = remote(own_out.at[ab], own_in.at[ab], own_send.at[ab], own_recv.at[ab], own_to)
        own_copies.append(copy)

        @pl.when(jnp.logical_not(own_self))
        def _():
            copy.start()

        @pl.when(own_self)
        def _():
            own_in[ab] = own_out[ab]

    def own_wait(ab):
        @pl.when(jnp.logical_not(own_self))
        def _():
            own_copies[ab].wait()

    dims = ((x, x_device), (y, y_device), (z, z_device))
    parts = []
    for where, size, home, order in (
        (0, 256, core * 512, (0, 1, 2)),
        (256, 256, core * 512 + 256, (1, 2, 0)),
        (512, 128, 1024 + core * 256, (2, 0, 1)),
        (640, 128, 1024 + core * 256 + 128, (1, 2, 0)),
    ):
        q = [dims[d][0] for d in order]
        parts.append((where, size, home, q, [dims[d][1] for d in order]))
    gram_copies = {}

    def gram_step(p, n):
        where, size, home, q, dev = parts[p]
        one, two = size // 4, size // 16
        row_1 = q[0] * one
        row_2 = row_1 + q[1] * two
        column = pl.ds(pl.multiple_of(q[2] * 128, 128), 128)
        if n > 0:
            for copy in gram_copies[p, n - 1]:
                copy.wait_recv()
        copies = []
        gram_copies[p, n] = copies
        if n == 0:
            pass
        elif n == 1:
            rows = rows_of(where + row_1, one)
            got = [gram_1[p, i, 0:one, :] for i in range(3)]
            gram_core[rows, :] += got[0] + got[1] + got[2]
        elif n == 2:
            rows = rows_of(where + row_2, two)
            got = [gram_2[p, i, 0:two, :] for i in range(3)]
            gram_core[rows, :] += got[0] + got[1] + got[2]
        elif n == 3:
            rows = rows_of(where + row_2, two)
            got = [gram_3[p, i, 0:two, :] for i in range(3)]
            out_g_ref[rows_of(home + row_2, two), column] = (
                gram_core[rows, column] + got[0] + got[1] + got[2]
            )
        for i, step in enumerate(steps):
            if n == 0:
                src = gram_core.at[rows_of(where + ((q[0] + step) % 4) * one, one), :]
                dst = gram_1.at[p, i, pl.ds(0, one), :]
            elif n == 1:
                src = gram_core.at[rows_of(where + row_1 + ((q[1] + step) % 4) * two, two), :]
                dst = gram_2.at[p, i, pl.ds(0, two), :]
            elif n == 2:
                to = pl.ds(pl.multiple_of(((q[2] + step) % 4) * 128, 128), 128)
                src = gram_core.at[rows_of(where + row_2, two), to]
                dst = gram_3.at[p, i, pl.ds(0, two), :]
            elif n == 3:
                src = dst = out_g_ref.at[rows_of(home + row_2, two), column]
            elif n == 4:
                src = dst = out_g_ref.at[rows_of(home + row_2, two), :]
            elif n == 5:
                src = dst = out_g_ref.at[rows_of(home + row_1, one), :]
            if n < 6:
                d = dev[n if n < 3 else 5 - n]
                copies.append(send(src, dst, gs_send.at[p, n, i], gs_recv.at[p, n, i], d(step)))
        if n == 6:
            src = dst = out_g_ref.at[rows_of(home, size), :]
            copies.append(send(src, dst, gg_send.at[p], gg_recv.at[p], mate))

    def gram_of(f, p):
        fh, fl = split(f)
        ph, low = split(p)
        return dot_tn(fh, ph) + (dot_tn(fh, low) + dot_tn(fl, ph))

    hits = lax.fori_loop(0, 8192 // tile, place, jnp.zeros((OWN, 128), F32))
    out_g_ref[pl.ds(3 * W + 2 * OWN, OWN), :] = jnp.broadcast_to(jnp.sum(hits, axis=1, keepdims=True), (OWN, W))
    far_a = gather_far(0)
    y_start(1)
    gather_near(0)
    far_a.wait_recv()
    near[0] += far_in[0]
    row_start(0)
    for i in range(3):
        pass_on(1, i)
    far_b = gather_far(1)
    row_turn(0, 0)
    gather_near(1)
    far_b.wait_recv()
    near[1] += far_in[1]
    row_turn(0, 1)
    row_start(1)
    row_end(0)
    product_out(0, 0)
    row_turn(1, 0)
    product_out(0, 1)
    product_own(0, 0)
    ring_start(0, 0)
    row_turn(1, 1)
    product_own(0, 1)
    ring_start(0, 1)
    own_start_copy(0)
    ring_turn(0, 0)
    ring_turn(0, 1)
    row_end(1)
    product_out(1, 0)
    product_out(1, 1)
    ring_across(0)
    product_own(1, 0)
    ring_start(1, 0)
    product_own(1, 1)
    ring_start(1, 1)
    own_start_copy(1)
    product_a = ring_end(0)
    ring_turn(1, 0)
    ring_turn(1, 1)
    own_wait(0)
    gram[0:W, :] = gram_of(own_in[0], product_a)
    own_wait(1)
    gram[W : 2 * W, :] = gram_of(own_in[1], product_a)
    core_a = send(
        gram.at[rows_of((1 - core) * W, W), :],
        gram_core.at[0:W, :],
        gc_send.at[0],
        gc_recv.at[0],
        mate,
    )
    core_a.wait_recv()
    gram_core[0:W, :] += gram[rows_of(core * W, W), :]
    gram_step(0, 0)
    gram_step(1, 0)
    ring_across(1)
    gram_step(0, 1)
    gram_step(1, 1)
    product_b = ring_end(1)
    gram[2 * W : 3 * W, :] = gram_of(own_in[1], product_b)
    core_b = send(
        gram.at[rows_of(2 * W + (1 - core) * 256, 256), :],
        gram_core.at[W : W + 256, :],
        gc_send.at[1],
        gc_recv.at[1],
        mate,
    )
    gram_step(0, 2)
    gram_step(1, 2)
    core_b.wait_recv()
    gram_core[W : W + 256, :] += gram[rows_of(2 * W + core * 256, 256), :]
    gram_step(2, 0)
    gram_step(3, 0)
    gram_step(0, 3)
    gram_step(1, 3)
    for n in range(1, 7):
        gram_step(2, n)
        gram_step(3, n)
        if n + 3 < 7:
            gram_step(0, n + 3)
            gram_step(1, n + 3)
    for p in range(4):
        gram_copies[p, 6][0].wait_recv()
    for copy in pending:
        copy.wait_send()


def final_kernel(
    g_ref, pivot_a_ref, top_ref, pivot_b_ref, ia_ref, da_ref, ib_ref, tb_ref, db_ref
):
    top = top_ref[...]
    product_a = g_ref[3 * W : 3 * W + OWN, :]
    product_b = g_ref[3 * W + OWN : 3 * W + 2 * OWN, :]
    selected = g_ref[3 * W + 2 * OWN :, :]
    ia_ref[...] = -product_a
    ib_ref[...] = -(product_b - dot3(product_a, top)) * selected
    diagonal_a = pivot_a_ref[...] + g_ref[:W, :]
    da_ref[...] = diagonal_a
    cross_neg_t = g_ref[W : 2 * W, :]
    cross_neg = cross_neg_t.T
    top_b = cross_neg - dot3(diagonal_a, top)
    tb_ref[...] = top_b
    top_t = top.T
    db_ref[...] = (
        pivot_b_ref[...] - dot3(top_t, top_b) + (g_ref[2 * W : 3 * W, :] - dot3(cross_neg_t, top))
    )


def body(
    inverse_block,
    grid_position,
    panel_a,
    pivot_inverse_a,
    chosen_rows,
    top_panel_b,
    panel_b,
    pivot_inverse_b,
):
    vmem = pl.BlockSpec(memory_space=pltpu.VMEM)
    dma = pltpu.SemaphoreType.DMA
    out = jax.ShapeDtypeStruct
    gp = grid_position.reshape(1, -1)
    gpt = grid_position.reshape(96, 128)
    gram = pl.pallas_call(
        main_kernel,
        out_shape=out((3 * W + 3 * OWN, W), F32),
        in_specs=[pl.BlockSpec(memory_space=pl.ANY)] + [vmem] * 5,
        out_specs=vmem,
        scratch_shapes=[
            pltpu.VMEM((1536, MA), F32),
            pltpu.VMEM((2, 768, MA), BF16),
            pltpu.VMEM((2, 768, MA), BF16),
            pltpu.VMEM((1, 8192), jnp.int32),
            pltpu.VMEM((8, FEAT, MA), F32),
            pltpu.VMEM((8, FEAT, MB), F32),
            pltpu.VMEM((2, FEAT, MA), F32),
            pltpu.VMEM((2, FEAT, MA), F32),
            pltpu.VMEM((2, FEAT, MA), F32),
            pltpu.VMEM((2, 8, FEAT, MA), F32),
            pltpu.VMEM((2, W, MA), BF16),
            pltpu.VMEM((2, W, MA), BF16),
            pltpu.VMEM((2, 768, W), F32),
            pltpu.VMEM((2, 768, W), F32),
            pltpu.VMEM((2, 768, W), F32),
            pltpu.VMEM((2, 2, 2, 48, W), F32),
            pltpu.VMEM((2, 2, 2, OWN, W), F32),
            pltpu.VMEM((2, OWN, W), F32),
            pltpu.VMEM((2, OWN, W), F32),
            pltpu.VMEM((2, OWN, W), F32),
            pltpu.VMEM((2, OWN, W), F32),
            pltpu.VMEM((3 * W, W), F32),
            pltpu.VMEM((3 * W // 2, W), F32),
            pltpu.VMEM((4, 3, 64, W), F32),
            pltpu.VMEM((4, 3, 16, W), F32),
            pltpu.VMEM((4, 3, 16, 128), F32),
            dma,
            dma((2, 3)),
            dma((2, 3)),
            dma((2, 4)),
            dma((2, 4)),
            dma((2,)),
            dma((2,)),
            dma((2, 9)),
            dma((2, 9)),
            dma((2, 2)),
            dma((2, 2)),
            dma((2, 2, 6)),
            dma((2, 2, 6)),
            dma((2,)),
            dma((2,)),
            dma((2,)),
            dma((2,)),
            dma((2,)),
            dma((2,)),
            dma((4, 6, 3)),
            dma((4, 6, 3)),
            dma((4,)),
            dma((4,)),
        ],
        compiler_params=pltpu.CompilerParams(
            collective_id=0, has_side_effects=True, vmem_limit_bytes=60 << 20
        ),
        cost_estimate=pl.CostEstimate(
            flops=10_000_000_000, bytes_accessed=20_000_000, transcendentals=0
        ),
        name="exchange",
    )(inverse_block, gp, gpt, chosen_rows.reshape(1, -1), panel_a, panel_b)
    return pl.pallas_call(
        final_kernel,
        out_shape=(
            out((OWN, W), F32),
            out((W, W), F32),
            out((OWN, W), F32),
            out((W, W), F32),
            out((W, W), F32),
        ),
        in_specs=[vmem] * 4,
        out_specs=(vmem,) * 5,
        compiler_params=pltpu.CompilerParams(vmem_limit_bytes=48 << 20),
        name="finish",
    )(gram, pivot_inverse_a, top_panel_b, pivot_inverse_b)


def solution(mesh):
    in_specs = (P("row", "col"), P(), P("row", "col"), P(), P(), P(), P("row", "col"), P())
    out_specs = (P(("row", "col"), None), P(), P(("row", "col"), None), P(), P())
    return jax.shard_map(body, mesh=mesh, in_specs=in_specs, out_specs=out_specs, check_vma=False)
```

```python
import functools

import jax
import jax.numpy as jnp
from jax import lax
from jax.experimental import pallas as pl
from jax.experimental.pallas import tpu as pltpu
from jax.sharding import PartitionSpec as P

MESH = pl.DeviceIdType.MESH
F32 = jnp.float32
BF16 = jnp.bfloat16
NT = (((1,), (1,)), ((), ()))
TN = (((0,), (0,)), ((), ()))
W = 512
FEAT = 64
MA = 768
MB = 512
OWN = 96


def split(x):
    high = x.astype(BF16)
    return high, (x - high.astype(F32)).astype(BF16)


def dot_nn(a, b):
    return jnp.dot(a, b, preferred_element_type=F32)


def dot_nt(a, b):
    return lax.dot_general(a, b, NT, preferred_element_type=F32)


def dot_tn(a, b):
    return lax.dot_general(a, b, TN, preferred_element_type=F32)


def dot3(a, b):
    ah, al = split(a)
    bh, bl = split(b)
    return dot_nn(ah, bh) + (dot_nn(ah, bl) + dot_nn(al, bh))


def remote(src, dst, send, recv, device):
    return pltpu.make_async_remote_copy(
        src_ref=src,
        dst_ref=dst,
        send_sem=send,
        recv_sem=recv,
        device_id=device,
        device_id_type=MESH,
    )


def main_kernel(
    block_ref,
    gp_ref,
    gpt_ref,
    chosen_ref,
    pa_ref,
    pb_ref,
    out_g_ref,
    b_f32,
    b_high,
    b_low,
    gb,
    xa,
    xb,
    near,
    far,
    far_in,
    full,
    full_high,
    full_low,
    half_out,
    half_in,
    half_own,
    ring_2,
    ring_1,
    x_out,
    x_in,
    own_out,
    own_in,
    own_far,
    gram,
    gram_core,
    gram_1,
    gram_2,
    gram_3,
    b_sem,
    y_send,
    y_recv,
    c_send,
    c_recv,
    far_send,
    far_recv,
    row_send,
    row_recv,
    half_send,
    half_recv,
    ring_send,
    ring_recv,
    x_send,
    x_recv,
    own_send,
    own_recv,
    gc_send,
    gc_recv,
    of_send,
    of_recv,
    gs_send,
    gs_recv,
    gg_send,
    gg_recv,
):
    r = lax.axis_index("row")
    c = lax.axis_index("col")
    x_lo, z = r // 4, r % 4
    x_hi, y, core = c // 8, (c // 2) % 4, c % 2
    x = x_hi * 2 + x_lo
    mate = (r, c + 1 - 2 * core)

    def x_device(dx):
        nx = (x + dx) % 4
        return ((nx % 2) * 4 + z, ((nx // 2) * 4 + y) * 2 + core)

    def y_device(dy):
        return (r, (x_hi * 4 + (y + dy) % 4) * 2 + core)

    def z_device(dz):
        return (x_lo * 4 + (z + dz) % 4, c)

    x_pair = ((1 - x_lo) * 4 + z, c)
    x_across = x_device(2)
    own_part = ((y + z) % 4) * 2 + x_lo
    own_to = (c // 2, core * 8 + own_part)
    own_from = (core * 4 + (y + 4 - z) % 4, 2 * r + x_hi)
    own_self = jnp.logical_and(own_to[0] == r, own_to[1] == c)
    pending = []

    def send(src, dst, send_sem, recv_sem, device):
        copy = remote(src, dst, send_sem, recv_sem, device)
        copy.start()
        pending.append(copy)
        return copy

    def rows_of(start, size):
        return pl.ds(pl.multiple_of(start, size), size)

    block_copy = pltpu.make_async_copy(block_ref, b_f32, b_sem)
    block_copy.start()

    barrier = pltpu.get_barrier_semaphore()

    def greet(device):
        pl.semaphore_signal(barrier, inc=1, device_id=device, device_id_type=MESH)

    greet(mate)
    for step in (1, 2, 3):
        greet(x_device(4 - step))
        greet(y_device(4 - step))
        greet(z_device(4 - step))

    @pl.when(jnp.logical_not(own_self))
    def _():
        greet(own_from)
        pl.semaphore_wait(barrier, 11)

    @pl.when(own_self)
    def _():
        pl.semaphore_wait(barrier, 10)

    mine = y * 2 + core
    steps = (1, 3, 2)
    panels = (pa_ref, pb_ref)
    held = (xa, xb)
    y_copies = [None, None]
    mate_copies = [None, None]

    def y_start(ab):
        mate_copies[ab] = [
            send(panels[ab], held[ab].at[mine], c_send.at[ab, 0], c_recv.at[ab, 0], mate)
        ]
        y_copies[ab] = [
            send(panels[ab], held[ab].at[mine], y_send.at[ab, i], y_recv.at[ab, i], y_device(dy))
            for i, dy in enumerate(steps)
        ]

    y_start(0)

    def pass_on(ab, i):
        slot = ((y + 4 - steps[i]) % 4) * 2 + core
        y_copies[ab][i].wait_recv()
        ref = held[ab].at[slot]
        mate_copies[ab].append(send(ref, ref, c_send.at[ab, i + 1], c_recv.at[ab, i + 1], mate))

    block_copy.wait()

    def divide(i, carry):
        high, low = split(b_f32[rows_of(i * OWN, OWN), :])
        b_high[i % 2, rows_of((i // 2) * OWN, OWN), :] = high
        b_low[i % 2, rows_of((i // 2) * OWN, OWN), :] = low
        return carry

    lax.fori_loop(0, 16, divide, 0)

    gpt = gpt_ref[...]
    table = jnp.concatenate([gpt >> 7, gpt & 127], axis=1).astype(F32).T.astype(BF16)
    own_start = r * (OWN * 16) + c * OWN
    tile = 1024

    def place(t, hits):
        ch = chosen_ref[:, rows_of(t * tile, tile)]
        pick = jnp.where(
            lax.broadcasted_iota(jnp.int32, (96, tile), 0) == (ch >> 7), 1.0, 0.0
        ).astype(BF16)
        found = dot_nn(table, pick)
        value = found[:128] * 128.0 + found[128:]
        value = jnp.where(
            lax.broadcasted_iota(jnp.int32, (128, tile), 0) == (ch & 127), value, 0.0
        )
        position = jnp.sum(value, axis=0, keepdims=True).astype(jnp.int32)
        gb[:, rows_of(t * tile, tile)] = position
        same = lax.broadcasted_iota(jnp.int32, (OWN, tile), 0) + own_start == position
        same = jnp.where(same, 1.0, 0.0)
        for i in range(tile // 128):
            hits = hits + same[:, i * 128 : (i + 1) * 128]
        return hits

    def take(panel, positions, first):
        width = panel.shape[1]
        hit = lax.broadcasted_iota(jnp.int32, (MA, width), 0) + first == positions
        hot = jnp.where(hit, 1.0, 0.0).astype(BF16)
        high, low = split(panel)
        both = dot_nt(jnp.concatenate([high, low], axis=0), hot)
        return both[:FEAT] + both[FEAT:]

    def gather(ab, slot, target, to_x):
        first = ((to_x * 4 + y) * 2 + core) * MA
        source = x_hi * 8 + slot
        if ab == 0:
            positions = gp_ref[:, pl.ds(pl.multiple_of(source * MA, 128), MA)]
        else:
            positions = gb[:, pl.ds(pl.multiple_of(source * MB, 128), MB)]
        target[ab] += take(held[ab][slot], positions, first)

    xa[mine] = pa_ref[...]
    xb[mine] = pb_ref[...]
    near[...] = jnp.zeros_like(near)
    far[...] = jnp.zeros_like(far)

    def gather_far(ab):
        gather(ab, mine, far, 1 - x_hi)
        mate_copies[ab][0].wait_recv()
        gather(ab, y * 2 + 1 - core, far, 1 - x_hi)
        for i, dy in enumerate(steps):
            base = ((y + 4 - dy) % 4) * 2
            if ab == 0:
                pass_on(ab, i)
            gather(ab, base + core, far, 1 - x_hi)
            mate_copies[ab][i + 1].wait_recv()
            gather(ab, base + 1 - core, far, 1 - x_hi)
        return send(far.at[ab], far_in.at[ab], far_send.at[ab], far_recv.at[ab], x_across)

    def gather_near(ab):
        def step(i, carry):
            gather(ab, i, near, x_hi)
            return carry

        lax.fori_loop(0, 8, step, 0)

    def store_full(ab, slot, value):
        high, low = split(value)
        full_high[ab, rows_of(slot * FEAT, FEAT), :] = high
        full_low[ab, rows_of(slot * FEAT, FEAT), :] = low

    row_copies = [{}, {}]
    sets = (x_lo, 1 - x_lo)

    def row_put(ab, name, src, slot, part, k, device):
        dst = full.at[ab, slot]
        if part is not None:
            dst = dst.at[pl.ds(part * 32, 32), :]
        row_copies[ab][name] = send(
            dst if src is None else src, dst, row_send.at[ab, k], row_recv.at[ab, k], device
        )

    def row_start(ab):
        src = near.at[ab]
        row_put(ab, "pair", src, r, None, 0, x_pair)
        row_put(ab, "up0", src, r, None, 1, z_device(1))
        row_put(ab, "down0", src, r, None, 2, z_device(3))
        store_full(ab, r, near[ab])

    def row_turn(ab, s):
        base = sets[s] * 4
        below = base + (z + 3) % 4
        above = base + (z + 1) % 4
        row_copies[ab]["up%d" % s].wait_recv()
        row_put(ab, "far_up%d" % s, None, below, 0, 3 + 4 * s, z_device(1))
        row_copies[ab]["down%d" % s].wait_recv()
        row_put(ab, "far_down%d" % s, None, above, 1, 4 + 4 * s, z_device(3))
        if s == 0:
            other = (1 - x_lo) * 4 + z
            row_copies[ab]["pair"].wait_recv()
            row_put(ab, "up1", None, other, None, 5, z_device(1))
            row_put(ab, "down1", None, other, None, 6, z_device(3))
            store_full(ab, other, full[ab, other])
        store_full(ab, below, full[ab, below])
        store_full(ab, above, full[ab, above])

    def row_end(ab):
        for s in range(2):
            slot = sets[s] * 4 + (z + 2) % 4
            row_copies[ab]["far_up%d" % s].wait_recv()
            row_copies[ab]["far_down%d" % s].wait_recv()
            store_full(ab, slot, full[ab, slot])

    halves = (1 - x_hi, x_hi)

    def multiply(ab, part, half, target):
        rows = rows_of(half * 384, 384)
        bh = b_high[part, rows, :]
        bl = b_low[part, rows, :]
        fh = full_high[ab]
        fl = full_low[ab]
        target[ab, rows, :] = dot_nt(bh, fh) + (dot_nt(bh, fl) + dot_nt(bl, fh))

    half_copies = [[None, None], [None, None]]

    def product_out(ab, s):
        rows = rows_of(halves[s] * 384, 384)
        multiply(ab, 1 - core, halves[s], half_out)
        half_copies[ab][s] = send(
            half_out.at[ab, rows, :],
            half_in.at[ab, rows, :],
            half_send.at[ab, s],
            half_recv.at[ab, s],
            mate,
        )

    def product_own(ab, s):
        rows = rows_of(halves[s] * 384, 384)
        multiply(ab, core, halves[s], half_own)
        half_copies[ab][s].wait_recv()
        half_own[ab, rows, :] += half_in[ab, rows, :]

    ring_copies = {}

    def chunk(s, dy, part=None):
        start = (halves[s] * 4 + (y + dy) % 4) * OWN
        if part is None:
            return rows_of(start, OWN)
        return rows_of(start + part * 48, 48)

    def ring_put(ab, s, name, k, src_rows, dst, device):
        ring_copies[ab, s, name] = send(
            half_own.at[ab, src_rows, :], dst, ring_send.at[ab, s, k], ring_recv.at[ab, s, k], device
        )

    low_part = pl.ds(0, 48)
    high_part = pl.ds(48, 48)

    def ring_start(ab, s):
        up, down = y_device(1), y_device(3)
        ring_put(ab, s, "two_up", 0, chunk(s, 2, 0), ring_2.at[ab, s, 0], up)
        ring_put(ab, s, "two_down", 1, chunk(s, 2, 1), ring_2.at[ab, s, 1], down)
        ring_put(ab, s, "up_high", 2, chunk(s, 1, 1), ring_1.at[ab, s, 0, high_part, :], up)
        ring_put(ab, s, "down_low", 3, chunk(s, 3, 0), ring_1.at[ab, s, 1, low_part, :], down)

    def ring_turn(ab, s):
        up, down = y_device(1), y_device(3)
        ring_copies[ab, s, "two_up"].wait_recv()
        half_own[ab, chunk(s, 1, 0), :] += ring_2[ab, s, 0]
        ring_put(ab, s, "up_low", 4, chunk(s, 1, 0), ring_1.at[ab, s, 0, low_part, :], up)
        ring_copies[ab, s, "two_down"].wait_recv()
        half_own[ab, chunk(s, 3, 1), :] += ring_2[ab, s, 1]
        ring_put(ab, s, "down_high", 5, chunk(s, 3, 1), ring_1.at[ab, s, 1, high_part, :], down)

    def ring_sum(ab, s):
        for name in ("up_high", "down_low", "up_low", "down_high"):
            ring_copies[ab, s, name].wait_recv()
        return half_own[ab, chunk(s, 0), :] + ring_1[ab, s, 0] + ring_1[ab, s, 1]

    def ring_across(ab):
        x_out[ab] = ring_sum(ab, 0)
        ring_copies[ab] = send(
            x_out.at[ab], x_in.at[ab], x_send.at[ab], x_recv.at[ab], x_across
        )

    def ring_end(ab, total=None):
        if total is None:
            total = ring_sum(ab, 1)
        ring_copies[ab].wait_recv()
        total = total + x_in[ab]
        out_g_ref[pl.ds(3 * W + ab * OWN, OWN), :] = total
        return total

    own_copies = []

    def own_start_copy(ab):
        line = lax.broadcasted_iota(jnp.int32, (OWN, MA), 0) + own_part * OWN
        pick = jnp.where(line == lax.broadcasted_iota(jnp.int32, (OWN, MA), 1), 1.0, 0.0)
        pick = pick.astype(BF16)
        own_out[ab] = dot_nt(pick, full_high[ab]) + dot_nt(pick, full_low[ab])
        copy = remote(own_out.at[ab], own_in.at[ab], own_send.at[ab], own_recv.at[ab], own_to)
        own_copies.append(copy)

        @pl.when(jnp.logical_not(own_self))
        def _():
            copy.start()

        @pl.when(own_self)
        def _():
            own_in[ab] = own_out[ab]

    def own_wait(ab):
        @pl.when(jnp.logical_not(own_self))
        def _():
            own_copies[ab].wait()

    dims = ((x, x_device), (y, y_device), (z, z_device))
    parts = []
    for where, size, home, order in (
        (0, 256, core * 512, (0, 1, 2)),
        (256, 256, core * 512 + 256, (1, 2, 0)),
        (512, 128, 1024 + core * 256, (2, 0, 1)),
        (640, 128, 1024 + core * 256 + 128, (1, 2, 0)),
    ):
        q = [dims[d][0] for d in order]
        parts.append((where, size, home, q, [dims[d][1] for d in order]))
    gram_copies = {}

    def gram_step(p, n):
        where, size, home, q, dev = parts[p]
        one, two = size // 4, size // 16
        row_1 = q[0] * one
        row_2 = row_1 + q[1] * two
        column = pl.ds(pl.multiple_of(q[2] * 128, 128), 128)
        if n > 0:
            for copy in gram_copies[p, n - 1]:
                copy.wait_recv()
        copies = []
        gram_copies[p, n] = copies
        if n == 0:
            pass
        elif n == 1:
            rows = rows_of(where + row_1, one)
            got = [gram_1[p, i, 0:one, :] for i in range(3)]
            gram_core[rows, :] += got[0] + got[1] + got[2]
        elif n == 2:
            rows = rows_of(where + row_2, two)
            got = [gram_2[p, i, 0:two, :] for i in range(3)]
            gram_core[rows, :] += got[0] + got[1] + got[2]
        elif n == 3:
            rows = rows_of(where + row_2, two)
            got = [gram_3[p, i, 0:two, :] for i in range(3)]
            out_g_ref[rows_of(home + row_2, two), column] = (
                gram_core[rows, column] + got[0] + got[1] + got[2]
            )
        for i, step in enumerate(steps):
            if n == 0:
                src = gram_core.at[rows_of(where + ((q[0] + step) % 4) * one, one), :]
                dst = gram_1.at[p, i, pl.ds(0, one), :]
            elif n == 1:
                src = gram_core.at[rows_of(where + row_1 + ((q[1] + step) % 4) * two, two), :]
                dst = gram_2.at[p, i, pl.ds(0, two), :]
            elif n == 2:
                to = pl.ds(pl.multiple_of(((q[2] + step) % 4) * 128, 128), 128)
                src = gram_core.at[rows_of(where + row_2, two), to]
                dst = gram_3.at[p, i, pl.ds(0, two), :]
            elif n == 3:
                src = dst = out_g_ref.at[rows_of(home + row_2, two), column]
            elif n == 4:
                src = dst = out_g_ref.at[rows_of(home + row_2, two), :]
            elif n == 5:
                src = dst = out_g_ref.at[rows_of(home + row_1, one), :]
            if n < 6:
                d = dev[n if n < 3 else 5 - n]
                copies.append(send(src, dst, gs_send.at[p, n, i], gs_recv.at[p, n, i], d(step)))
        if n == 6:
            src = dst = out_g_ref.at[rows_of(home, size), :]
            copies.append(send(src, dst, gg_send.at[p], gg_recv.at[p], mate))

    def gram_of(f, p):
        fh, fl = split(f)
        ph, low = split(p)
        return dot_tn(fh, ph) + (dot_tn(fh, low) + dot_tn(fl, ph))

    hits = lax.fori_loop(0, 8192 // tile, place, jnp.zeros((OWN, 128), F32))
    out_g_ref[pl.ds(3 * W + 2 * OWN, OWN), :] = jnp.broadcast_to(jnp.sum(hits, axis=1, keepdims=True), (OWN, W))
    far_a = gather_far(0)
    y_start(1)
    gather_near(0)
    far_a.wait_recv()
    near[0] += far_in[0]
    row_start(0)
    for i in range(3):
        pass_on(1, i)
    far_b = gather_far(1)
    row_turn(0, 0)
    gather_near(1)
    far_b.wait_recv()
    near[1] += far_in[1]
    row_turn(0, 1)
    row_start(1)
    row_end(0)
    product_out(0, 0)
    row_turn(1, 0)
    product_out(0, 1)
    product_own(0, 0)
    ring_start(0, 0)
    row_turn(1, 1)
    product_own(0, 1)
    ring_start(0, 1)
    own_start_copy(0)
    ring_turn(0, 0)
    ring_turn(0, 1)
    row_end(1)
    product_out(1, 0)
    product_out(1, 1)
    ring_across(0)
    product_own(1, 0)
    ring_start(1, 0)
    product_own(1, 1)
    ring_start(1, 1)
    own_start_copy(1)
    product_a = ring_end(0)
    ring_turn(1, 0)
    ring_turn(1, 1)
    own_wait(1)
    own_across = send(own_in.at[1], own_far, of_send, of_recv, x_across)
    own_wait(0)
    gram[0:W, :] = gram_of(own_in[0], product_a)
    gram[W : 2 * W, :] = gram_of(own_in[1], product_a)
    core_a = send(
        gram.at[rows_of((1 - core) * W, W), :],
        gram_core.at[0:W, :],
        gc_send.at[0],
        gc_recv.at[0],
        mate,
    )
    ring_across(1)
    core_a.wait_recv()
    gram_core[0:W, :] += gram[rows_of(core * W, W), :]
    gram_step(0, 0)
    gram_step(1, 0)
    total_b = ring_sum(1, 1)
    own_across.wait_recv()
    gram[2 * W : 3 * W, :] = gram_of(
        jnp.concatenate([own_in[1], own_far[...]], axis=0),
        jnp.concatenate([total_b, x_out[1]], axis=0),
    )
    core_b = send(
        gram.at[rows_of(2 * W + (1 - core) * 256, 256), :],
        gram_core.at[W : W + 256, :],
        gc_send.at[1],
        gc_recv.at[1],
        mate,
    )
    core_b.wait_recv()
    gram_core[W : W + 256, :] += gram[rows_of(2 * W + core * 256, 256), :]
    gram_step(2, 0)
    gram_step(3, 0)
    gram_step(2, 1)
    gram_step(3, 1)
    ring_end(1, total_b)
    gram_step(0, 1)
    gram_step(1, 1)
    gram_step(2, 2)
    gram_step(3, 2)
    gram_step(0, 2)
    gram_step(1, 2)
    gram_step(2, 3)
    gram_step(3, 3)
    gram_step(0, 3)
    gram_step(1, 3)
    gram_step(2, 4)
    gram_step(3, 4)
    gram_step(0, 4)
    gram_step(1, 4)
    gram_step(2, 5)
    gram_step(3, 5)
    gram_step(0, 5)
    gram_step(1, 5)
    gram_step(2, 6)
    gram_step(3, 6)
    gram_step(0, 6)
    gram_step(1, 6)
    for p in range(4):
        gram_copies[p, 6][0].wait_recv()
    for copy in pending:
        copy.wait_send()


def final_kernel(
    g_ref, pivot_a_ref, top_ref, pivot_b_ref, ia_ref, da_ref, ib_ref, tb_ref, db_ref
):
    top = top_ref[...]
    product_a = g_ref[3 * W : 3 * W + OWN, :]
    product_b = g_ref[3 * W + OWN : 3 * W + 2 * OWN, :]
    selected = g_ref[3 * W + 2 * OWN :, :]
    ia_ref[...] = -product_a
    ib_ref[...] = -(product_b - dot3(product_a, top)) * selected
    diagonal_a = pivot_a_ref[...] + g_ref[:W, :]
    da_ref[...] = diagonal_a
    cross_neg_t = g_ref[W : 2 * W, :]
    cross_neg = cross_neg_t.T
    top_b = cross_neg - dot3(diagonal_a, top)
    tb_ref[...] = top_b
    top_t = top.T
    db_ref[...] = (
        pivot_b_ref[...] - dot3(top_t, top_b) + (g_ref[2 * W : 3 * W, :] - dot3(cross_neg_t, top))
    )


def body(
    inverse_block,
    grid_position,
    panel_a,
    pivot_inverse_a,
    chosen_rows,
    top_panel_b,
    panel_b,
    pivot_inverse_b,
):
    vmem = pl.BlockSpec(memory_space=pltpu.VMEM)
    dma = pltpu.SemaphoreType.DMA
    out = jax.ShapeDtypeStruct
    gp = grid_position.reshape(1, -1)
    gpt = grid_position.reshape(96, 128)
    gram = pl.pallas_call(
        main_kernel,
        out_shape=out((3 * W + 3 * OWN, W), F32),
        in_specs=[pl.BlockSpec(memory_space=pl.ANY)] + [vmem] * 5,
        out_specs=vmem,
        scratch_shapes=[
            pltpu.VMEM((1536, MA), F32),
            pltpu.VMEM((2, 768, MA), BF16),
            pltpu.VMEM((2, 768, MA), BF16),
            pltpu.VMEM((1, 8192), jnp.int32),
            pltpu.VMEM((8, FEAT, MA), F32),
            pltpu.VMEM((8, FEAT, MB), F32),
            pltpu.VMEM((2, FEAT, MA), F32),
            pltpu.VMEM((2, FEAT, MA), F32),
            pltpu.VMEM((2, FEAT, MA), F32),
            pltpu.VMEM((2, 8, FEAT, MA), F32),
            pltpu.VMEM((2, W, MA), BF16),
            pltpu.VMEM((2, W, MA), BF16),
            pltpu.VMEM((2, 768, W), F32),
            pltpu.VMEM((2, 768, W), F32),
            pltpu.VMEM((2, 768, W), F32),
            pltpu.VMEM((2, 2, 2, 48, W), F32),
            pltpu.VMEM((2, 2, 2, OWN, W), F32),
            pltpu.VMEM((2, OWN, W), F32),
            pltpu.VMEM((2, OWN, W), F32),
            pltpu.VMEM((2, OWN, W), F32),
            pltpu.VMEM((2, OWN, W), F32),
            pltpu.VMEM((OWN, W), F32),
            pltpu.VMEM((3 * W, W), F32),
            pltpu.VMEM((3 * W // 2, W), F32),
            pltpu.VMEM((4, 3, 64, W), F32),
            pltpu.VMEM((4, 3, 16, W), F32),
            pltpu.VMEM((4, 3, 16, 128), F32),
            dma,
            dma((2, 3)),
            dma((2, 3)),
            dma((2, 4)),
            dma((2, 4)),
            dma((2,)),
            dma((2,)),
            dma((2, 9)),
            dma((2, 9)),
            dma((2, 2)),
            dma((2, 2)),
            dma((2, 2, 6)),
            dma((2, 2, 6)),
            dma((2,)),
            dma((2,)),
            dma((2,)),
            dma((2,)),
            dma((2,)),
            dma((2,)),
            dma,
            dma,
            dma((4, 6, 3)),
            dma((4, 6, 3)),
            dma((4,)),
            dma((4,)),
        ],
        compiler_params=pltpu.CompilerParams(
            collective_id=0, has_side_effects=True, vmem_limit_bytes=60 << 20
        ),
        cost_estimate=pl.CostEstimate(
            flops=10_000_000_000, bytes_accessed=20_000_000, transcendentals=0
        ),
        name="exchange",
    )(inverse_block, gp, gpt, chosen_rows.reshape(1, -1), panel_a, panel_b)
    return pl.pallas_call(
        final_kernel,
        out_shape=(
            out((OWN, W), F32),
            out((W, W), F32),
            out((OWN, W), F32),
            out((W, W), F32),
            out((W, W), F32),
        ),
        in_specs=[vmem] * 4,
        out_specs=(vmem,) * 5,
        compiler_params=pltpu.CompilerParams(vmem_limit_bytes=48 << 20),
        name="finish",
    )(gram, pivot_inverse_a, top_panel_b, pivot_inverse_b)


def solution(mesh):
    in_specs = (P("row", "col"), P(), P("row", "col"), P(), P(), P(), P("row", "col"), P())
    out_specs = (P(("row", "col"), None), P(), P(("row", "col"), None), P(), P())
    return jax.shard_map(body, mesh=mesh, in_specs=in_specs, out_specs=out_specs, check_vma=False)
```

```python
import functools

import jax
import jax.numpy as jnp
from jax import lax
from jax.experimental import pallas as pl
from jax.experimental.pallas import tpu as pltpu
from jax.sharding import PartitionSpec as P

MESH = pl.DeviceIdType.MESH
F32 = jnp.float32
BF16 = jnp.bfloat16
NT = (((1,), (1,)), ((), ()))
TN = (((0,), (0,)), ((), ()))
W = 512
FEAT = 64
MA = 768
MB = 512
OWN = 96


def split(x):
    high = x.astype(BF16)
    return high, (x - high.astype(F32)).astype(BF16)


def dot_nn(a, b):
    return jnp.dot(a, b, preferred_element_type=F32)


def dot_nt(a, b):
    return lax.dot_general(a, b, NT, preferred_element_type=F32)


def dot_tn(a, b):
    return lax.dot_general(a, b, TN, preferred_element_type=F32)


def dot3(a, b):
    ah, al = split(a)
    bh, bl = split(b)
    return dot_nn(ah, bh) + (dot_nn(ah, bl) + dot_nn(al, bh))


def remote(src, dst, send, recv, device):
    return pltpu.make_async_remote_copy(
        src_ref=src,
        dst_ref=dst,
        send_sem=send,
        recv_sem=recv,
        device_id=device,
        device_id_type=MESH,
    )


def main_kernel(
    block_ref,
    gp_ref,
    gpt_ref,
    chosen_ref,
    pa_ref,
    pb_ref,
    out_g_ref,
    b_f32,
    b_high,
    b_low,
    gb,
    xa,
    xb,
    near,
    far,
    far_in,
    full,
    full_high,
    full_low,
    half_out,
    half_in,
    half_own,
    ring_2,
    ring_1,
    x_out,
    x_in,
    own_out,
    own_in,
    own_far,
    gram,
    gram_core,
    gram_1,
    gram_2,
    gram_3,
    b_sem,
    y_send,
    y_recv,
    c_send,
    c_recv,
    far_send,
    far_recv,
    row_send,
    row_recv,
    half_send,
    half_recv,
    ring_send,
    ring_recv,
    x_send,
    x_recv,
    own_send,
    own_recv,
    gc_send,
    gc_recv,
    of_send,
    of_recv,
    gs_send,
    gs_recv,
    gg_send,
    gg_recv,
):
    r = lax.axis_index("row")
    c = lax.axis_index("col")
    x_lo, z = r // 4, r % 4
    x_hi, y, core = c // 8, (c // 2) % 4, c % 2
    x = x_hi * 2 + x_lo
    mate = (r, c + 1 - 2 * core)

    def x_device(dx):
        nx = (x + dx) % 4
        return ((nx % 2) * 4 + z, ((nx // 2) * 4 + y) * 2 + core)

    def y_device(dy):
        return (r, (x_hi * 4 + (y + dy) % 4) * 2 + core)

    def z_device(dz):
        return (x_lo * 4 + (z + dz) % 4, c)

    x_pair = ((1 - x_lo) * 4 + z, c)
    x_across = x_device(2)
    own_part = ((y + z) % 4) * 2 + x_lo
    own_to = (c // 2, core * 8 + own_part)
    own_from = (core * 4 + (y + 4 - z) % 4, 2 * r + x_hi)
    own_self = jnp.logical_and(own_to[0] == r, own_to[1] == c)
    pending = []

    def send(src, dst, send_sem, recv_sem, device):
        copy = remote(src, dst, send_sem, recv_sem, device)
        copy.start()
        pending.append(copy)
        return copy

    def rows_of(start, size):
        return pl.ds(pl.multiple_of(start, size), size)

    block_copy = pltpu.make_async_copy(block_ref, b_f32, b_sem)
    block_copy.start()

    barrier = pltpu.get_barrier_semaphore()

    def greet(device):
        pl.semaphore_signal(barrier, inc=1, device_id=device, device_id_type=MESH)

    greet(mate)
    for step in (1, 2, 3):
        greet(x_device(4 - step))
        greet(y_device(4 - step))
        greet(z_device(4 - step))

    @pl.when(jnp.logical_not(own_self))
    def _():
        greet(own_from)
        pl.semaphore_wait(barrier, 11)

    @pl.when(own_self)
    def _():
        pl.semaphore_wait(barrier, 10)

    mine = y * 2 + core
    steps = (1, 3, 2)
    panels = (pa_ref, pb_ref)
    held = (xa, xb)
    y_copies = [None, None]
    mate_copies = [None, None]

    def y_start(ab):
        mate_copies[ab] = [
            send(panels[ab], held[ab].at[mine], c_send.at[ab, 0], c_recv.at[ab, 0], mate)
        ]
        y_copies[ab] = [
            send(panels[ab], held[ab].at[mine], y_send.at[ab, i], y_recv.at[ab, i], y_device(dy))
            for i, dy in enumerate(steps)
        ]

    y_start(0)

    def pass_on(ab, i):
        slot = ((y + 4 - steps[i]) % 4) * 2 + core
        y_copies[ab][i].wait_recv()
        ref = held[ab].at[slot]
        mate_copies[ab].append(send(ref, ref, c_send.at[ab, i + 1], c_recv.at[ab, i + 1], mate))

    block_copy.wait()

    def divide(i, carry):
        high, low = split(b_f32[rows_of(i * OWN, OWN), :])
        b_high[i % 2, rows_of((i // 2) * OWN, OWN), :] = high
        b_low[i % 2, rows_of((i // 2) * OWN, OWN), :] = low
        return carry

    lax.fori_loop(0, 16, divide, 0)

    gpt = gpt_ref[...]
    table = jnp.concatenate([gpt >> 7, gpt & 127], axis=1).astype(F32).T.astype(BF16)
    own_start = r * (OWN * 16) + c * OWN
    tile = 1024

    def place(t, hits):
        ch = chosen_ref[:, rows_of(t * tile, tile)]
        pick = jnp.where(
            lax.broadcasted_iota(jnp.int32, (96, tile), 0) == (ch >> 7), 1.0, 0.0
        ).astype(BF16)
        found = dot_nn(table, pick)
        value = found[:128] * 128.0 + found[128:]
        value = jnp.where(
            lax.broadcasted_iota(jnp.int32, (128, tile), 0) == (ch & 127), value, 0.0
        )
        position = jnp.sum(value, axis=0, keepdims=True).astype(jnp.int32)
        gb[:, rows_of(t * tile, tile)] = position
        same = lax.broadcasted_iota(jnp.int32, (OWN, tile), 0) + own_start == position
        same = jnp.where(same, 1.0, 0.0)
        for i in range(tile // 128):
            hits = hits + same[:, i * 128 : (i + 1) * 128]
        return hits

    def take(panel, positions, first):
        width = panel.shape[1]
        hit = lax.broadcasted_iota(jnp.int32, (MA, width), 0) + first == positions
        hot = jnp.where(hit, 1.0, 0.0).astype(BF16)
        high, low = split(panel)
        both = dot_nt(jnp.concatenate([high, low], axis=0), hot)
        return both[:FEAT] + both[FEAT:]

    def gather(ab, slot, target, to_x):
        first = ((to_x * 4 + y) * 2 + core) * MA
        source = x_hi * 8 + slot
        if ab == 0:
            positions = gp_ref[:, pl.ds(pl.multiple_of(source * MA, 128), MA)]
        else:
            positions = gb[:, pl.ds(pl.multiple_of(source * MB, 128), MB)]
        target[ab] += take(held[ab][slot], positions, first)

    xa[mine] = pa_ref[...]
    xb[mine] = pb_ref[...]
    near[...] = jnp.zeros_like(near)
    far[...] = jnp.zeros_like(far)

    def gather_far(ab):
        gather(ab, mine, far, 1 - x_hi)
        mate_copies[ab][0].wait_recv()
        gather(ab, y * 2 + 1 - core, far, 1 - x_hi)
        for i, dy in enumerate(steps):
            base = ((y + 4 - dy) % 4) * 2
            if ab == 0:
                pass_on(ab, i)
            if ab == 0 and i == 2:
                y_start(1)
            gather(ab, base + core, far, 1 - x_hi)
            mate_copies[ab][i + 1].wait_recv()
            gather(ab, base + 1 - core, far, 1 - x_hi)
        return send(far.at[ab], far_in.at[ab], far_send.at[ab], far_recv.at[ab], x_across)

    def gather_near(ab):
        def step(i, carry):
            gather(ab, i, near, x_hi)
            return carry

        lax.fori_loop(0, 8, step, 0)

    def store_full(ab, slot, value):
        high, low = split(value)
        full_high[ab, rows_of(slot * FEAT, FEAT), :] = high
        full_low[ab, rows_of(slot * FEAT, FEAT), :] = low

    row_copies = [{}, {}]
    sets = (x_lo, 1 - x_lo)

    def row_put(ab, name, src, slot, part, k, device):
        dst = full.at[ab, slot]
        if part is not None:
            dst = dst.at[pl.ds(part * 32, 32), :]
        row_copies[ab][name] = send(
            dst if src is None else src, dst, row_send.at[ab, k], row_recv.at[ab, k], device
        )

    def row_start(ab):
        src = near.at[ab]
        row_put(ab, "pair", src, r, None, 0, x_pair)
        row_put(ab, "up0", src, r, None, 1, z_device(1))
        row_put(ab, "down0", src, r, None, 2, z_device(3))
        store_full(ab, r, near[ab])

    def row_turn(ab, s):
        base = sets[s] * 4
        below = base + (z + 3) % 4
        above = base + (z + 1) % 4
        if s == 0:
            other = (1 - x_lo) * 4 + z
            row_copies[ab]["pair"].wait_recv()
            row_put(ab, "up1", None, other, None, 5, z_device(1))
            row_put(ab, "down1", None, other, None, 6, z_device(3))
        row_copies[ab]["up%d" % s].wait_recv()
        row_put(ab, "far_up%d" % s, None, below, 0, 3 + 4 * s, z_device(1))
        row_copies[ab]["down%d" % s].wait_recv()
        row_put(ab, "far_down%d" % s, None, above, 1, 4 + 4 * s, z_device(3))
        if s == 0:
            store_full(ab, other, full[ab, other])
        store_full(ab, below, full[ab, below])
        store_full(ab, above, full[ab, above])

    def row_end(ab):
        for s in range(2):
            slot = sets[s] * 4 + (z + 2) % 4
            row_copies[ab]["far_up%d" % s].wait_recv()
            row_copies[ab]["far_down%d" % s].wait_recv()
            store_full(ab, slot, full[ab, slot])

    halves = (1 - x_hi, x_hi)

    def multiply(ab, part, half, target):
        rows = rows_of(half * 384, 384)
        bh = b_high[part, rows, :]
        bl = b_low[part, rows, :]
        fh = full_high[ab]
        fl = full_low[ab]
        target[ab, rows, :] = dot_nt(bh, fh) + (dot_nt(bh, fl) + dot_nt(bl, fh))

    half_copies = [[None, None], [None, None]]

    def product_out(ab, s):
        rows = rows_of(halves[s] * 384, 384)
        multiply(ab, 1 - core, halves[s], half_out)
        half_copies[ab][s] = send(
            half_out.at[ab, rows, :],
            half_in.at[ab, rows, :],
            half_send.at[ab, s],
            half_recv.at[ab, s],
            mate,
        )

    def product_own(ab, s):
        rows = rows_of(halves[s] * 384, 384)
        multiply(ab, core, halves[s], half_own)
        half_copies[ab][s].wait_recv()
        half_own[ab, rows, :] += half_in[ab, rows, :]

    ring_copies = {}

    def chunk(s, dy, part=None):
        start = (halves[s] * 4 + (y + dy) % 4) * OWN
        if part is None:
            return rows_of(start, OWN)
        return rows_of(start + part * 48, 48)

    def ring_put(ab, s, name, k, src_rows, dst, device):
        ring_copies[ab, s, name] = send(
            half_own.at[ab, src_rows, :], dst, ring_send.at[ab, s, k], ring_recv.at[ab, s, k], device
        )

    low_part = pl.ds(0, 48)
    high_part = pl.ds(48, 48)

    def ring_start(ab, s):
        up, down = y_device(1), y_device(3)
        ring_put(ab, s, "two_up", 0, chunk(s, 2, 0), ring_2.at[ab, s, 0], up)
        ring_put(ab, s, "two_down", 1, chunk(s, 2, 1), ring_2.at[ab, s, 1], down)
        ring_put(ab, s, "up_high", 2, chunk(s, 1, 1), ring_1.at[ab, s, 0, high_part, :], up)
        ring_put(ab, s, "down_low", 3, chunk(s, 3, 0), ring_1.at[ab, s, 1, low_part, :], down)

    def ring_turn(ab, s):
        up, down = y_device(1), y_device(3)
        ring_copies[ab, s, "two_up"].wait_recv()
        half_own[ab, chunk(s, 1, 0), :] += ring_2[ab, s, 0]
        ring_put(ab, s, "up_low", 4, chunk(s, 1, 0), ring_1.at[ab, s, 0, low_part, :], up)
        ring_copies[ab, s, "two_down"].wait_recv()
        half_own[ab, chunk(s, 3, 1), :] += ring_2[ab, s, 1]
        ring_put(ab, s, "down_high", 5, chunk(s, 3, 1), ring_1.at[ab, s, 1, high_part, :], down)

    def ring_sum(ab, s):
        for name in ("up_high", "down_low", "up_low", "down_high"):
            ring_copies[ab, s, name].wait_recv()
        return half_own[ab, chunk(s, 0), :] + ring_1[ab, s, 0] + ring_1[ab, s, 1]

    def ring_across(ab):
        x_out[ab] = ring_sum(ab, 0)
        ring_copies[ab] = send(
            x_out.at[ab], x_in.at[ab], x_send.at[ab], x_recv.at[ab], x_across
        )

    def ring_end(ab, total=None):
        if total is None:
            total = ring_sum(ab, 1)
        ring_copies[ab].wait_recv()
        total = total + x_in[ab]
        out_g_ref[pl.ds(3 * W + ab * OWN, OWN), :] = total
        return total

    own_copies = []

    def own_start_copy(ab):
        line = lax.broadcasted_iota(jnp.int32, (OWN, MA), 0) + own_part * OWN
        pick = jnp.where(line == lax.broadcasted_iota(jnp.int32, (OWN, MA), 1), 1.0, 0.0)
        pick = pick.astype(BF16)
        own_out[ab] = dot_nt(pick, full_high[ab]) + dot_nt(pick, full_low[ab])
        copy = remote(own_out.at[ab], own_in.at[ab], own_send.at[ab], own_recv.at[ab], own_to)
        own_copies.append(copy)

        @pl.when(jnp.logical_not(own_self))
        def _():
            copy.start()

        @pl.when(own_self)
        def _():
            own_in[ab] = own_out[ab]

    def own_wait(ab):
        @pl.when(jnp.logical_not(own_self))
        def _():
            own_copies[ab].wait()

    dims = ((x, x_device), (y, y_device), (z, z_device))
    parts = []
    for where, size, home, order in (
        (0, 256, core * 512, (0, 1, 2)),
        (256, 256, core * 512 + 256, (1, 2, 0)),
        (512, 128, 1024 + core * 256, (2, 0, 1)),
        (640, 128, 1024 + core * 256 + 128, (1, 2, 0)),
    ):
        q = [dims[d][0] for d in order]
        parts.append((where, size, home, q, [dims[d][1] for d in order]))
    gram_copies = {}

    def gram_step(p, n):
        where, size, home, q, dev = parts[p]
        one, two = size // 4, size // 16
        row_1 = q[0] * one
        row_2 = row_1 + q[1] * two
        column = pl.ds(pl.multiple_of(q[2] * 128, 128), 128)
        if n > 0:
            for copy in gram_copies[p, n - 1]:
                copy.wait_recv()
        copies = []
        gram_copies[p, n] = copies
        if n == 0:
            pass
        elif n == 1:
            rows = rows_of(where + row_1, one)
            got = [gram_1[p, i, 0:one, :] for i in range(3)]
            gram_core[rows, :] += got[0] + got[1] + got[2]
        elif n == 2:
            rows = rows_of(where + row_2, two)
            got = [gram_2[p, i, 0:two, :] for i in range(3)]
            gram_core[rows, :] += got[0] + got[1] + got[2]
        elif n == 3:
            rows = rows_of(where + row_2, two)
            got = [gram_3[p, i, 0:two, :] for i in range(3)]
            out_g_ref[rows_of(home + row_2, two), column] = (
                gram_core[rows, column] + got[0] + got[1] + got[2]
            )
        for i, step in enumerate(steps):
            if n == 0:
                src = gram_core.at[rows_of(where + ((q[0] + step) % 4) * one, one), :]
                dst = gram_1.at[p, i, pl.ds(0, one), :]
            elif n == 1:
                src = gram_core.at[rows_of(where + row_1 + ((q[1] + step) % 4) * two, two), :]
                dst = gram_2.at[p, i, pl.ds(0, two), :]
            elif n == 2:
                to = pl.ds(pl.multiple_of(((q[2] + step) % 4) * 128, 128), 128)
                src = gram_core.at[rows_of(where + row_2, two), to]
                dst = gram_3.at[p, i, pl.ds(0, two), :]
            elif n == 3:
                src = dst = out_g_ref.at[rows_of(home + row_2, two), column]
            elif n == 4:
                src = dst = out_g_ref.at[rows_of(home + row_2, two), :]
            elif n == 5:
                src = dst = out_g_ref.at[rows_of(home + row_1, one), :]
            if n < 6:
                d = dev[n if n < 3 else 5 - n]
                copies.append(send(src, dst, gs_send.at[p, n, i], gs_recv.at[p, n, i], d(step)))
        if n == 6:
            src = dst = out_g_ref.at[rows_of(home, size), :]
            copies.append(send(src, dst, gg_send.at[p], gg_recv.at[p], mate))

    def gram_of(f, p):
        fh, fl = split(f)
        ph, low = split(p)
        return dot_tn(fh, ph) + (dot_tn(fh, low) + dot_tn(fl, ph))

    hits = lax.fori_loop(0, 8192 // tile, place, jnp.zeros((OWN, 128), F32))
    out_g_ref[pl.ds(3 * W + 2 * OWN, OWN), :] = jnp.broadcast_to(jnp.sum(hits, axis=1, keepdims=True), (OWN, W))
    far_a = gather_far(0)
    gather_near(0)
    far_a.wait_recv()
    near[0] += far_in[0]
    row_start(0)
    for i in range(3):
        pass_on(1, i)
    far_b = gather_far(1)
    row_turn(0, 0)
    gather_near(1)
    far_b.wait_recv()
    near[1] += far_in[1]
    row_turn(0, 1)
    row_start(1)
    row_end(0)
    product_out(0, 0)
    row_turn(1, 0)
    product_out(0, 1)
    product_own(0, 0)
    ring_start(0, 0)
    row_turn(1, 1)
    product_own(0, 1)
    ring_start(0, 1)
    own_start_copy(0)
    ring_turn(0, 0)
    ring_turn(0, 1)
    row_end(1)
    product_out(1, 0)
    product_out(1, 1)
    ring_across(0)
    product_own(1, 0)
    ring_start(1, 0)
    product_own(1, 1)
    ring_start(1, 1)
    own_start_copy(1)
    product_a = ring_end(0)
    ring_turn(1, 0)
    ring_turn(1, 1)
    own_wait(1)
    own_across = send(own_in.at[1], own_far, of_send, of_recv, x_across)
    own_wait(0)
    gram[0:W, :] = gram_of(own_in[0], product_a)
    gram[W : 2 * W, :] = gram_of(own_in[1], product_a)
    core_a = send(
        gram.at[rows_of((1 - core) * W, W), :],
        gram_core.at[0:W, :],
        gc_send.at[0],
        gc_recv.at[0],
        mate,
    )
    ring_across(1)
    core_a.wait_recv()
    gram_core[0:W, :] += gram[rows_of(core * W, W), :]
    gram_step(0, 0)
    gram_step(1, 0)
    total_b = ring_sum(1, 1)
    own_across.wait_recv()
    gram[2 * W : 3 * W, :] = gram_of(
        jnp.concatenate([own_in[1], own_far[...]], axis=0),
        jnp.concatenate([total_b, x_out[1]], axis=0),
    )
    core_b = send(
        gram.at[rows_of(2 * W + (1 - core) * 256, 256), :],
        gram_core.at[W : W + 256, :],
        gc_send.at[1],
        gc_recv.at[1],
        mate,
    )
    core_b.wait_recv()
    gram_core[W : W + 256, :] += gram[rows_of(2 * W + core * 256, 256), :]
    gram_step(2, 0)
    gram_step(3, 0)
    gram_step(2, 1)
    gram_step(3, 1)
    ring_end(1, total_b)
    gram_step(0, 1)
    gram_step(1, 1)
    gram_step(2, 2)
    gram_step(3, 2)
    gram_step(0, 2)
    gram_step(1, 2)
    gram_step(2, 3)
    gram_step(3, 3)
    gram_step(0, 3)
    gram_step(1, 3)
    gram_step(2, 4)
    gram_step(3, 4)
    gram_step(0, 4)
    gram_step(1, 4)
    gram_step(2, 5)
    gram_step(3, 5)
    gram_step(0, 5)
    gram_step(1, 5)
    gram_step(2, 6)
    gram_step(3, 6)
    gram_step(0, 6)
    gram_step(1, 6)
    for p in range(4):
        gram_copies[p, 6][0].wait_recv()
    for copy in pending:
        copy.wait_send()


def final_kernel(
    g_ref, pivot_a_ref, top_ref, pivot_b_ref, ia_ref, da_ref, ib_ref, tb_ref, db_ref
):
    top = top_ref[...]
    product_a = g_ref[3 * W : 3 * W + OWN, :]
    product_b = g_ref[3 * W + OWN : 3 * W + 2 * OWN, :]
    selected = g_ref[3 * W + 2 * OWN :, :]
    ia_ref[...] = -product_a
    ib_ref[...] = -(product_b - dot3(product_a, top)) * selected
    diagonal_a = pivot_a_ref[...] + g_ref[:W, :]
    da_ref[...] = diagonal_a
    cross_neg_t = g_ref[W : 2 * W, :]
    cross_neg = cross_neg_t.T
    top_b = cross_neg - dot3(diagonal_a, top)
    tb_ref[...] = top_b
    top_t = top.T
    db_ref[...] = (
        pivot_b_ref[...] - dot3(top_t, top_b) + (g_ref[2 * W : 3 * W, :] - dot3(cross_neg_t, top))
    )


def body(
    inverse_block,
    grid_position,
    panel_a,
    pivot_inverse_a,
    chosen_rows,
    top_panel_b,
    panel_b,
    pivot_inverse_b,
):
    vmem = pl.BlockSpec(memory_space=pltpu.VMEM)
    dma = pltpu.SemaphoreType.DMA
    out = jax.ShapeDtypeStruct
    gp = grid_position.reshape(1, -1)
    gpt = grid_position.reshape(96, 128)
    gram = pl.pallas_call(
        main_kernel,
        out_shape=out((3 * W + 3 * OWN, W), F32),
        in_specs=[pl.BlockSpec(memory_space=pl.ANY)] + [vmem] * 5,
        out_specs=vmem,
        scratch_shapes=[
            pltpu.VMEM((1536, MA), F32),
            pltpu.VMEM((2, 768, MA), BF16),
            pltpu.VMEM((2, 768, MA), BF16),
            pltpu.VMEM((1, 8192), jnp.int32),
            pltpu.VMEM((8, FEAT, MA), F32),
            pltpu.VMEM((8, FEAT, MB), F32),
            pltpu.VMEM((2, FEAT, MA), F32),
            pltpu.VMEM((2, FEAT, MA), F32),
            pltpu.VMEM((2, FEAT, MA), F32),
            pltpu.VMEM((2, 8, FEAT, MA), F32),
            pltpu.VMEM((2, W, MA), BF16),
            pltpu.VMEM((2, W, MA), BF16),
            pltpu.VMEM((2, 768, W), F32),
            pltpu.VMEM((2, 768, W), F32),
            pltpu.VMEM((2, 768, W), F32),
            pltpu.VMEM((2, 2, 2, 48, W), F32),
            pltpu.VMEM((2, 2, 2, OWN, W), F32),
            pltpu.VMEM((2, OWN, W), F32),
            pltpu.VMEM((2, OWN, W), F32),
            pltpu.VMEM((2, OWN, W), F32),
            pltpu.VMEM((2, OWN, W), F32),
            pltpu.VMEM((OWN, W), F32),
            pltpu.VMEM((3 * W, W), F32),
            pltpu.VMEM((3 * W // 2, W), F32),
            pltpu.VMEM((4, 3, 64, W), F32),
            pltpu.VMEM((4, 3, 16, W), F32),
            pltpu.VMEM((4, 3, 16, 128), F32),
            dma,
            dma((2, 3)),
            dma((2, 3)),
            dma((2, 4)),
            dma((2, 4)),
            dma((2,)),
            dma((2,)),
            dma((2, 9)),
            dma((2, 9)),
            dma((2, 2)),
            dma((2, 2)),
            dma((2, 2, 6)),
            dma((2, 2, 6)),
            dma((2,)),
            dma((2,)),
            dma((2,)),
            dma((2,)),
            dma((2,)),
            dma((2,)),
            dma,
            dma,
            dma((4, 6, 3)),
            dma((4, 6, 3)),
            dma((4,)),
            dma((4,)),
        ],
        compiler_params=pltpu.CompilerParams(
            collective_id=0, has_side_effects=True, vmem_limit_bytes=60 << 20
        ),
        cost_estimate=pl.CostEstimate(
            flops=10_000_000_000, bytes_accessed=20_000_000, transcendentals=0
        ),
        name="exchange",
    )(inverse_block, gp, gpt, chosen_rows.reshape(1, -1), panel_a, panel_b)
    return pl.pallas_call(
        final_kernel,
        out_shape=(
            out((OWN, W), F32),
            out((W, W), F32),
            out((OWN, W), F32),
            out((W, W), F32),
            out((W, W), F32),
        ),
        in_specs=[vmem] * 4,
        out_specs=(vmem,) * 5,
        compiler_params=pltpu.CompilerParams(vmem_limit_bytes=48 << 20),
        name="finish",
    )(gram, pivot_inverse_a, top_panel_b, pivot_inverse_b)


def solution(mesh):
    in_specs = (P("row", "col"), P(), P("row", "col"), P(), P(), P(), P("row", "col"), P())
    out_specs = (P(("row", "col"), None), P(), P(("row", "col"), None), P(), P())
    return jax.shard_map(body, mesh=mesh, in_specs=in_specs, out_specs=out_specs, check_vma=False)
```
